128 devices in a mesh: dp: 8 (over x_hi, y), expert: 16 (over z, x_lo, core).
Axes of the slice: x: 4 (x_hi: 2, x_lo: 2; x = x_hi * 2 + x_lo), y: 4, z: 4, core: 2. Of those that a mesh axis runs over, the one named last changes fastest.
Arguments:
- tokens: bfloat16 [32768, 2048], P(('dp', 'expert')), may hold values from -24 to 24
- cotangent: bfloat16 [32768, 2048], P(('dp', 'expert')), may hold values from -6 to 6
- route_gates: float32 [32768, 2], P(('dp', 'expert')), may hold values from 0.2 to 1
- w_gate_up: bfloat16 [16, 2048, 1536], P('expert'), may hold values from -0.125 to 0.125
- w_down: bfloat16 [16, 768, 2048], P('expert'), may hold values from -0.21875 to 0.21875
- expert_ids: int32 [32768, 2], P(('dp', 'expert')), may hold values from 0 to 15, as said below
- dest_ranks: int32 [32768, 2], P(('dp', 'expert')), may hold values from 0 to 15, as said below
- slot_ids: int32 [32768, 2], P(('dp', 'expert')), may hold values from -1 to 19, as said below
Outputs:
- mixed: bfloat16 [32768, 2048], P(('dp', 'expert'))
- token_grad: bfloat16 [32768, 2048], P(('dp', 'expert'))
- grad_gate_up: float32 [16, 2048, 1536], P('expert', 'dp')
- grad_down: float32 [16, 768, 2048], P('expert', 'dp')
The draws below stay inside these ranges and needn't reach their ends.
Inputs may be any that keep to these rules, and one draw needn't show every extreme that they name: `expert_ids`: the 2 routes of a token name different experts. `dest_ranks`: each route's serving device is its expert's own index or, for one hot expert that is the same for all tokens, one of 4 helper devices, the same for all tokens and different from the hot expert's own. `slot_ids`: A served route's row lies in the block that its token's device fills for one serving device and one copy (home or replica); no two routes of one device share a row of one block. For the hot expert, every device fills each of its blocks, at home and at every helper, with 20 routes.
All inputs are finite; a program needn't handle non-finite values.
Results may differ from the reference program's by a relative error of at most 0.015.
Values may be sent and summed in bfloat16 or wider, within the bound.
No kernel may reach another device: no remote copies, remote signals or barrier semaphores. Data moves between devices by JAX's collectives and lax.ppermute only.
A program may use at most 192 MiB of HBM per device.

```python
import jax
import jax.numpy as jnp
from jax import lax

D = 2048
FF = 768
TOP = 2
TOK_DEV = 256
EXPERTS = 16
TOKENS = 32768
CAP = 20
HELP = 4


def routing(key):
    key = jax.random.fold_in(key, 7)
    subkeys = jax.random.split(key, 7)
    blocks = TOKENS // TOK_DEV
    forced_count = (1 + HELP) * CAP
    hot_expert = jax.random.randint(subkeys[0], (), 0, EXPERTS, dtype=jnp.int32)
    steps_out = jnp.arange(HELP, dtype=jnp.int32)
    offsets = jnp.where(steps_out == 0, 1, EXPERTS // 2 + steps_out - 1).astype(jnp.int32)
    helpers = ((hot_expert + offsets) % EXPERTS).astype(jnp.int32)
    owners = jnp.concatenate([hot_expert[None], helpers]).astype(jnp.int32)
    live_rows = jax.random.randint(subkeys[2], (blocks,), 3 * TOK_DEV // 4, TOK_DEV + 1, dtype=jnp.int32)
    full_block = jax.random.randint(subkeys[3], (), 0, blocks, dtype=jnp.int32)
    live_rows = live_rows.at[full_block].set(TOK_DEV)
    orderings = jax.vmap(lambda sub: jax.random.permutation(sub, TOK_DEV))(jax.random.split(subkeys[4], blocks)).astype(jnp.int32)
    alive_perm = (orderings < live_rows[:, None]).astype(jnp.int32)
    rank_perm = jnp.cumsum(alive_perm, axis=1) * alive_perm
    rows_idx = jnp.arange(blocks, dtype=jnp.int32)[:, None]
    rank_tok = jnp.zeros((blocks, TOK_DEV), jnp.int32).at[rows_idx, orderings].set(rank_perm)
    forced = (rank_tok >= 1) & (rank_tok <= forced_count)
    position = jnp.arange(TOK_DEV, dtype=jnp.int32)[None, :]
    alive_tok = position < live_rows[:, None]
    pick_rand = (hot_expert + 1 + jax.random.randint(subkeys[5], (blocks, TOK_DEV), 0, EXPERTS - 1, dtype=jnp.int32)) % EXPERTS
    stride_pick = jax.random.randint(subkeys[6], (blocks, TOK_DEV), 0, EXPERTS - 2, dtype=jnp.int32)
    first_route = jnp.where(forced, hot_expert, pick_rand)
    offset = (first_route - hot_expert - 1) % EXPERTS
    second_free = (hot_expert + 1 + (offset + 1 + stride_pick) % (EXPERTS - 1)) % EXPERTS
    second_route = jnp.where(forced, pick_rand, second_free)
    route_ids = jnp.stack([first_route, second_route], axis=-1).astype(jnp.int32)
    owner_slot = jnp.maximum(rank_tok - 1, 0)
    forced_dest = owners[owner_slot % (1 + HELP)]
    forced_slot = owner_slot // (1 + HELP)
    forced_route = jnp.stack([forced, jnp.zeros_like(forced)], axis=-1)
    open_route = alive_tok[..., None] & jnp.logical_not(forced_route)
    flat_ids = route_ids.reshape(blocks, TOK_DEV * 2)
    flat_open = open_route.reshape(blocks, TOK_DEV * 2)
    expert_hits = ((flat_ids[..., None] == jnp.arange(EXPERTS, dtype=jnp.int32)[None, None, :]) & flat_open[..., None]).astype(jnp.int32)
    arrival = jnp.sum(jnp.cumsum(expert_hits, axis=1) * expert_hits, axis=2) - 1
    free_slot = jnp.where(flat_open & (arrival < CAP), arrival, -1).reshape(blocks, TOK_DEV, 2)
    slot_table = jnp.where(forced_route, forced_slot[..., None], free_slot).astype(jnp.int32)
    dest_table = jnp.where(forced_route, forced_dest[..., None], route_ids).astype(jnp.int32)
    return (route_ids.reshape(TOKENS, 2), dest_table.reshape(TOKENS, 2), slot_table.reshape(TOKENS, 2))


def draw_expert_ids(key, part):
    return routing(key)[0]


def draw_dest_ranks(key, part):
    return routing(key)[1]


def draw_slot_ids(key, part):
    return routing(key)[2]


def raised(values, key, source, target, blocks, factor):
    def block_of(axis_at):
        return (jnp.arange(values.shape[axis_at]) // (values.shape[axis_at] // blocks)).reshape((-1,) + (1,) * (values.ndim - 1 - axis_at))

    one_side = jax.random.permutation(key, blocks)[block_of(target)]
    far = (block_of(target) + blocks // 2) % blocks
    return jnp.where((block_of(source) == one_side) | (block_of(source) == far), factor * values, values)


def level_of(own_key, shape, cuts, low, largest):
    gain, own = 1.0, jax.random.fold_in(own_key, 6)
    for dim, blocks in cuts:
        steps = jnp.exp(jax.random.uniform(jax.random.fold_in(own, dim), (blocks,), jnp.float32, low / len(cuts), largest / len(cuts)))
        gain = gain * jnp.repeat(steps, shape[dim] // blocks).reshape([-1 if axis == dim else 1 for axis in range(len(shape))])
    return gain


def normal_values(key, dims, width, most, pieces=(), kind=jnp.bfloat16):
    factor_of = level_of(key, dims, pieces, -0.22, 0.18) if pieces else 1.0
    array = jax.random.normal(key, dims, jnp.float32) * width * factor_of
    return jnp.minimum(jnp.maximum(array, -most), most).astype(kind)


def bell_draw_with(stream_key, shape, width, bound, shards, heavy, kind=jnp.bfloat16):
    array = width * jax.random.normal(stream_key, shape, jnp.float32)
    if shards:
        array = array * level_of(stream_key, shape, shards, -0.22, 0.18)
    return jnp.clip(raised(array, jax.random.fold_in(stream_key, 3), *heavy), -bound, bound).astype(kind)


def setup_inputs(seed: int = 0) -> dict:
    key_of = jax.random.split(jax.random.key(seed), 9)
    tokens = bell_draw_with(key_of[0], (TOKENS, D), 1.0, 24.0, ((0, 128),), (0, 1, 128, 5.5))
    cotangent = normal_values(key_of[1], (TOKENS, D), 1.0, 6.0, ((0, 128),))
    route_gates = jnp.clip(0.2 + 0.8 * jax.random.uniform(key_of[2], (TOKENS, TOP), jnp.float32) ** level_of(key_of[2], (TOKENS, TOP), ((0, 128),), -0.2, 0.2), 0.2, 1.0)
    w_gate_up = normal_values(key_of[3], (EXPERTS, D, 2 * FF), D ** -0.5, 0.125, ((0, 16),))
    w_down = normal_values(key_of[4], (EXPERTS, FF, D), FF ** -0.5, 0.21875, ((0, 16),))
    expert_ids = draw_expert_ids(jax.random.fold_in(key_of[8], 71), 0)
    dest_ranks = draw_dest_ranks(jax.random.fold_in(key_of[8], 71), 0)
    slot_ids = draw_slot_ids(jax.random.fold_in(key_of[8], 71), 0)
    return {"tokens": tokens, "cotangent": cotangent, "route_gates": route_gates, "w_gate_up": w_gate_up, "w_down": w_down, "expert_ids": expert_ids, "dest_ranks": dest_ranks, "slot_ids": slot_ids}


def swiglu_pass(rows_in, rows_cot, weight_in, weight_out):
    unit_count = weight_out.shape[0]
    hidden = jnp.dot(rows_in, weight_in, preferred_element_type=jnp.float32)
    gate_part = hidden[:, :unit_count]
    up_part = hidden[:, unit_count:]
    sig_gate = jax.nn.sigmoid(gate_part)
    silu_gate = gate_part * sig_gate
    active = (silu_gate * up_part).astype(jnp.bfloat16)
    expert_out = jnp.dot(active, weight_out, preferred_element_type=jnp.float32).astype(jnp.bfloat16)
    grad_active = lax.dot_general(rows_cot, weight_out, (((1,), (1,)), ((), ())), preferred_element_type=jnp.float32)
    grad_out = lax.dot_general(active, rows_cot, (((0,), (0,)), ((), ())), preferred_element_type=jnp.float32).astype(jnp.bfloat16)
    grad_gate_act = grad_active * up_part * sig_gate * (1.0 + gate_part * (1.0 - sig_gate))
    grad_up_act = grad_active * silu_gate
    grad_hidden = jnp.concatenate([grad_gate_act, grad_up_act], axis=1).astype(jnp.bfloat16)
    back_rows = lax.dot_general(grad_hidden, weight_in, (((1,), (1,)), ((), ())), preferred_element_type=jnp.float32).astype(jnp.bfloat16)
    grad_in = lax.dot_general(rows_in, grad_hidden, (((0,), (0,)), ((), ())), preferred_element_type=jnp.float32).astype(jnp.bfloat16)
    return expert_out, back_rows, grad_in, grad_out


def reference(tokens, cotangent, route_gates, w_gate_up, w_down, expert_ids, dest_ranks, slot_ids):
    groups = TOKENS // (TOK_DEV * EXPERTS)
    model_width = tokens.shape[1]
    served = slot_ids >= 0
    hot_expert = jnp.max(jnp.where(served & (expert_ids != dest_ranks), expert_ids, -1)).astype(jnp.int32)
    token_index = jnp.arange(TOKENS, dtype=jnp.int32)
    block_id = token_index // TOK_DEV
    source_rank = (block_id % EXPERTS)[:, None]
    copy_flag = (expert_ids != dest_ranks).astype(jnp.int32)
    group_len = EXPERTS * 2 * EXPERTS * CAP
    local_pos = ((dest_ranks * 2 + copy_flag) * EXPERTS + source_rank) * CAP + slot_ids
    global_pos = jnp.where(served, (block_id // EXPERTS)[:, None] * group_len + local_pos, groups * group_len)
    route_index = jnp.arange(TOKENS * TOP, dtype=jnp.int32)
    route_table = jnp.full((groups * group_len,), -1, jnp.int32).at[global_pos.reshape(-1)].set(route_index, mode="drop")
    route_table = route_table.reshape(groups, EXPERTS, 2, EXPERTS * CAP)
    gate_flat = route_gates.reshape(-1)
    hot_in = w_gate_up[hot_expert]
    hot_out = w_down[hot_expert]
    devices = jnp.arange(EXPERTS, dtype=jnp.int32)
    group_pos = jnp.where(served, local_pos, 0).astype(jnp.int32).reshape(groups, EXPERTS * TOK_DEV, TOP)
    group_served = served.reshape(groups, EXPERTS * TOK_DEV, TOP)
    group_gates = route_gates.reshape(groups, EXPERTS * TOK_DEV, TOP)

    def per_device(device_args):
        dev_table, device = device_args
        filled = dev_table >= 0
        source = jnp.where(filled, dev_table, 0).astype(jnp.int32)
        token_rows = source // TOP
        rows_in = jnp.where(filled[..., None], tokens[token_rows], jnp.zeros((), tokens.dtype)).astype(jnp.bfloat16)
        scaled = gate_flat[source][..., None] * cotangent[token_rows].astype(jnp.float32)
        rows_cot = jnp.where(filled[..., None], scaled, jnp.float32(0.0)).astype(jnp.bfloat16)
        home_part = swiglu_pass(rows_in[0], rows_cot[0], w_gate_up[device], w_down[device])
        replica_part = swiglu_pass(rows_in[1], rows_cot[1], hot_in, hot_out)
        out_rows = jnp.stack([home_part[0], replica_part[0]])
        back_rows = jnp.stack([home_part[1], replica_part[1]])
        return (out_rows, back_rows, home_part[2].astype(jnp.float32), home_part[3].astype(jnp.float32),
                replica_part[2].astype(jnp.float32), replica_part[3].astype(jnp.float32))

    def per_group(totals, inputs):
        acc_in, acc_out, spare_in, spare_out = totals
        group_table, positions, served_mask, gate_rows = inputs
        out_rows, back_rows, home_in, home_out, rep_in, rep_out = lax.map(per_device, (group_table, devices))
        out_flat = out_rows.reshape(-1, model_width)
        back_flat = back_rows.reshape(-1, model_width)
        weights = jnp.where(served_mask, gate_rows, jnp.float32(0.0))
        picked_out = out_flat[positions].astype(jnp.float32)
        mixed = jnp.sum(weights[..., None] * picked_out, axis=1).astype(jnp.bfloat16)
        picked_back = jnp.where(served_mask[..., None], back_flat[positions].astype(jnp.float32), jnp.float32(0.0))
        token_grad = jnp.sum(picked_back, axis=1).astype(jnp.bfloat16)
        totals = (acc_in + home_in, acc_out + home_out, spare_in + jnp.sum(rep_in, axis=0), spare_out + jnp.sum(rep_out, axis=0))
        return totals, (mixed, token_grad)

    start = (jnp.zeros(w_gate_up.shape, jnp.float32), jnp.zeros(w_down.shape, jnp.float32),
             jnp.zeros(w_gate_up.shape[1:], jnp.float32), jnp.zeros(w_down.shape[1:], jnp.float32))
    totals, (mixed, token_grad) = lax.scan(per_group, start, (route_table, group_pos, group_served, group_gates))
    acc_in, acc_out, spare_in, spare_out = totals
    grad_gate_up = acc_in.at[hot_expert].add(spare_in)
    grad_down = acc_out.at[hot_expert].add(spare_out)
    return (mixed.reshape(TOKENS, model_width), token_grad.reshape(TOKENS, model_width), grad_gate_up, grad_down)
```

```python
import jax
import jax.numpy as jnp
from jax import lax
from jax.experimental import pallas as pl
from jax.experimental.pallas import tpu as pltpu
from jax.sharding import PartitionSpec as P

AXES = ("dp", "expert")
BF = jnp.bfloat16
F32 = jnp.float32


def hop(x, dh=0, dy=0, dz=0, dl=0, dc=0):
    pairs = []
    for i in range(128):
        dp, ex = divmod(i, 16)
        h, y = divmod(dp, 4)
        z, l, c = ex // 4, (ex // 2) % 2, ex % 2
        j_dp = ((h + dh) % 2) * 4 + (y + dy) % 4
        j_ex = ((z + dz) % 4) * 4 + ((l + dl) % 2) * 2 + (c + dc) % 2
        pairs.append((i, j_dp * 16 + j_ex))
    return lax.ppermute(x, AXES, pairs)


def at(x, i, axis=0):
    return lax.dynamic_index_in_dim(x, i, axis, keepdims=False)


def dot(a, b, ca=1, cb=0):
    return lax.dot_general(a, b, (((ca,), (cb,)), ((), ())), preferred_element_type=F32)


def gather4(x, k, name):
    parts = [x] + [hop(x, **{name: s}) for s in (1, 2, 3)]
    out = jnp.zeros((4,) + x.shape, x.dtype)
    for s in range(4):
        out = lax.dynamic_update_index_in_dim(out, parts[s], (k - s) % 4, 0)
    return out


def scatter4(x, k, name, axis, dtype):
    got = [hop(at(x, (k + s) % 4, axis), **{name: s}) for s in (1, 2, 3)]
    own = at(x, k, axis).astype(F32)
    return (own + got[0].astype(F32) + got[1].astype(F32) + got[2].astype(F32)).astype(dtype)


def pair_sum(x, k, name, dtype):
    got = hop(at(x, 1 - k), **{name: 1})
    return (at(x, k).astype(F32) + got.astype(F32)).astype(dtype)


def both(own, other, k):
    return jnp.where(k == 0, jnp.stack([own, other]), jnp.stack([other, own]))


def pack_kernel(pos_ref, gate_ref, tok_ref, cot_ref, send_ref, hot_ref):
    tile = 512

    def select(rows, shift):
        row = lax.broadcasted_iota(jnp.int32, (rows, 256), 0) + shift
        m0 = row == pos_ref[0:1, :]
        m1 = row == pos_ref[1:2, :]
        pick = jnp.where(m0 | m1, 1.0, 0.0).astype(BF)
        gate = jnp.where(m0, gate_ref[0:1, :], 0.0) + jnp.where(m1, gate_ref[1:2, :], 0.0)
        return pick, jnp.sum(gate, axis=1, keepdims=True)

    home_x, _ = select(640, 0)
    home_g, home_gate = select(640, -20)
    hot_x, hot_gate = select(80, 640)
    for j in range(tok_ref.shape[1] // tile):
        cols = pl.ds(j * tile, tile)
        tok = tok_ref[:, cols]
        cot = cot_ref[:, cols]
        rows = dot(home_x, tok) + home_gate * dot(home_g, cot)
        send_ref[:, cols] = rows.astype(BF)
        hot_ref[0:80, cols] = dot(hot_x, tok).astype(BF)
        hot_ref[80:160, cols] = (hot_gate * dot(hot_x, cot)).astype(BF)


def pack(pos_t, gate_t, tokens, cotangent):
    width = tokens.shape[1]
    return pl.pallas_call(
        pack_kernel,
        out_shape=(
            jax.ShapeDtypeStruct((640, width), BF),
            jax.ShapeDtypeStruct((160, width), BF),
        ),
        compiler_params=pltpu.CompilerParams(vmem_limit_bytes=40 * 2**20),
        cost_estimate=pl.CostEstimate(flops=2 * 10**9, bytes_accessed=6 * 10**6, transcendentals=0),
        name="pack_rows",
    )(pos_t, gate_t, tokens, cotangent)


def unpack_kernel(pos_ref, gate_ref, ret_ref, hot_ref, mixed_ref, grad_ref):
    tile = 512

    def select(k, width, shift):
        column = lax.broadcasted_iota(jnp.int32, (256, width), 1) + shift
        return jnp.where(column == pos_ref[:, k : k + 1], 1.0, 0.0).astype(BF)

    out0, out1 = select(0, 640, 0), select(1, 640, 0)
    back = select(0, 640, -20) + select(1, 640, -20)
    hot0, hot1 = select(0, 80, 640), select(1, 80, 640)
    hot_back = hot0 + hot1
    gate0, gate1 = gate_ref[:, 0:1], gate_ref[:, 1:2]
    for j in range(ret_ref.shape[1] // tile):
        cols = pl.ds(j * tile, tile)
        ret = ret_ref[:, cols]
        hot_out = hot_ref[0:80, cols]
        first = dot(out0, ret) + dot(hot0, hot_out)
        second = dot(out1, ret) + dot(hot1, hot_out)
        mixed_ref[:, cols] = (gate0 * first + gate1 * second).astype(BF)
        total = dot(back, ret) + dot(hot_back, hot_ref[80:160, cols])
        grad_ref[:, cols] = total.astype(BF)


def unpack(pos, gates, returned, hot_rows):
    width = returned.shape[1]
    return pl.pallas_call(
        unpack_kernel,
        out_shape=(jax.ShapeDtypeStruct((256, width), BF),) * 2,
        compiler_params=pltpu.CompilerParams(vmem_limit_bytes=40 * 2**20),
        cost_estimate=pl.CostEstimate(flops=2 * 10**9, bytes_accessed=6 * 10**6, transcendentals=0),
        name="unpack_rows",
    )(pos, gates, returned, hot_rows)


def activations(hidden, grad_active, units):
    gate, up = hidden[:, :units], hidden[:, units:]
    sig = jax.nn.sigmoid(gate)
    silu = gate * sig
    active = (silu * up).astype(BF)
    grad_gate = grad_active * up * sig * (1.0 + gate * (1.0 - sig))
    grad_hidden = jnp.concatenate([grad_gate, grad_active * silu], axis=1).astype(BF)
    return active, grad_hidden


def shards(tokens, cotangent, route_gates, w_gate_up, w_down, expert_ids, dest_ranks, slot_ids):
    dp, ex = lax.axis_index("dp"), lax.axis_index("expert")
    h, y = dp // 4, dp % 4
    z, l, c = ex // 4, (ex // 2) % 2, ex % 2
    w_in, w_out = w_gate_up[0], w_down[0]

    served = slot_ids >= 0
    replica = served & (expert_ids != dest_ranks)
    hot = jnp.max(jnp.where(replica, expert_ids, -1))
    ranks = jnp.arange(16, dtype=jnp.int32)
    helps = jnp.any((dest_ranks[:, :, None] == ranks) & replica[:, :, None], axis=(0, 1))
    order = jnp.sum((helps & (ranks < dest_ranks[:, :, None])).astype(jnp.int32), axis=2)
    pos = jnp.where(replica, 640 + order * 20 + slot_ids, dest_ranks * 40 + slot_ids)
    pos = jnp.where(served, pos, -1000)
    hz, hl, hc = hot // 4, (hot // 2) % 2, hot % 2

    rows_in = lax.dynamic_slice(w_in, (256 * dp, 0), (256, 1536)).reshape(256, 2, 2, 384)
    rows_out = lax.dynamic_slice(w_out, (0, 256 * dp), (768, 256)).reshape(2, 384, 256)

    def half(k):
        part = at(rows_in, k, 2)
        return jnp.concatenate([part[:, 0], part[:, 1], at(rows_out, k).T], axis=1)

    got = hop(half(1 - c), dc=1)
    piece = jnp.where(c == hc, half(c), got).reshape(2, 128, 1152)
    got = hop(at(piece, 1 - l), dl=1)
    piece = jnp.where(l == hl, at(piece, l), got).reshape(4, 32, 1152)
    got = [hop(at(piece, (z + s) % 4), dz=s) for s in (1, 2, 3)]
    away = (z - hz) % 4
    piece = jnp.where(
        away == 0,
        at(piece, z),
        jnp.where(away == 1, got[0], jnp.where(away == 2, got[1], got[2])),
    )
    piece = gather4(piece, z, "dz").reshape(128, 1152)
    piece = both(piece, hop(piece, dl=1), l).reshape(256, 1152)
    piece = both(piece, hop(piece, dh=1), h)
    hot_w = gather4(piece, y, "dy").transpose(1, 0, 2, 3).reshape(2048, 1152)
    hot_in, hot_out = hot_w[:, :768], hot_w[:, 768:]

    send, hot_rows = pack(pos.T, route_gates.T, tokens, cotangent)
    recv = lax.all_to_all(send, "expert", split_axis=0, concat_axis=0, tiled=True)
    other_rows = hop(hot_rows, dc=1)

    row = jnp.arange(640, dtype=jnp.int32)
    compact = jnp.arange(320, dtype=jnp.int32)
    spread = compact // 20 * 40 + compact % 20
    pick_x = (spread[:, None] == row).astype(BF)
    pick_g = (spread[:, None] + 20 == row).astype(BF)
    rows_x = dot(pick_x, recv).astype(BF)
    rows_g = dot(pick_g, recv).astype(BF)
    hidden = dot(rows_x, w_in)
    grad_active = dot(rows_g, w_out, 1, 1)
    active, grad_hidden = activations(hidden, grad_active, 768)
    home_down = dot(active, rows_g, 0, 0).astype(BF)
    home_in = dot(rows_x, grad_hidden, 0, 0).astype(BF)
    expert_out = dot(active, w_out).astype(BF)
    back_rows = dot(grad_hidden, w_in, 1, 1).astype(BF)
    result = dot(
        jnp.concatenate([pick_x, pick_g], axis=0), jnp.concatenate([expert_out, back_rows]), 0, 0
    ).astype(BF)
    returned = lax.all_to_all(result, "expert", split_axis=0, concat_axis=0, tiled=True)

    home_in = scatter4(home_in.reshape(2, 4, 256, 1536), y, "dy", 1, BF)
    home_in = pair_sum(home_in, h, "dh", F32)
    home_down = pair_sum(home_down.reshape(2, 4, 96, 2048), h, "dh", BF)
    home_down = scatter4(home_down, y, "dy", 0, F32)

    rows_x = jnp.concatenate([hot_rows[:80], other_rows[:80]])
    rows_g = jnp.concatenate([hot_rows[80:], other_rows[80:]])
    hidden = dot(rows_x, hot_in)
    grad_active = dot(rows_g, hot_out)
    active, grad_hidden = activations(hidden, grad_active, 384)
    hot_grad_in = dot(rows_x, grad_hidden, 0, 0).astype(BF)
    hot_grad_down = dot(active, rows_g, 0, 0).astype(BF)
    part_out = dot(active, hot_out, 1, 1)
    part_back = dot(grad_hidden, hot_in, 1, 1)
    mine = jnp.concatenate([part_out[:80], part_back[:80]])
    theirs = jnp.concatenate([part_out[80:], part_back[80:]]).astype(BF)
    hot_result = (mine + hop(theirs, dc=1).astype(F32)).astype(BF)
    mixed, token_grad = unpack(pos, route_gates, returned, hot_result)

    spare_in = scatter4(hot_grad_in.reshape(2, 4, 4, 64, 768), z, "dz", 2, BF)
    spare_down = scatter4(hot_grad_down.reshape(4, 4, 24, 2048), z, "dz", 1, BF)
    spare_in = scatter4(spare_in, y, "dy", 1, BF)
    spare_down = scatter4(spare_down, y, "dy", 0, BF)
    spare_in = pair_sum(spare_in, h, "dh", BF)
    spare_down = (spare_down.astype(F32) + hop(spare_down, dh=1).astype(F32)).astype(BF)
    spare_in = (spare_in.astype(F32) + hop(spare_in, dl=1).astype(F32)).astype(BF)
    spare_down = (spare_down.astype(F32) + hop(spare_down, dl=1).astype(F32)).astype(BF)
    spare_in = gather4(spare_in, z, "dz").reshape(256, 768)
    spare_down = gather4(spare_down, z, "dz").reshape(96, 2048)
    halves = both(spare_in, hop(spare_in, dc=1), c).reshape(2, 256, 2, 384)
    spare_in = halves.transpose(1, 2, 0, 3).reshape(256, 1536)
    spare_down = jnp.where(c == h, spare_down, hop(spare_down, dc=1))
    is_home = ex == hot
    grad_gate_up = home_in + jnp.where(is_home, spare_in.astype(F32), 0.0)
    grad_down = home_down + jnp.where(is_home, spare_down.astype(F32), 0.0)
    return mixed, token_grad, grad_gate_up[None], grad_down[None]


def solution(mesh):
    rows = P(AXES, None)
    weights = P("expert", None, None)
    grads = P("expert", "dp", None)
    return jax.shard_map(
        shards,
        mesh=mesh,
        in_specs=(rows, rows, rows, weights, weights, rows, rows, rows),
        out_specs=(rows, rows, grads, grads),
        check_vma=False,
    )
```

```python
import functools

import jax
import jax.numpy as jnp
from jax import lax
from jax.experimental import pallas as pl
from jax.experimental.pallas import tpu as pltpu
from jax.sharding import PartitionSpec as P

AXES = ("dp", "expert")
BF = jnp.bfloat16
F32 = jnp.float32


def hop(x, dh=0, dy=0, dz=0, dl=0, dc=0):
    pairs = []
    for i in range(128):
        dp, ex = divmod(i, 16)
        h, y = divmod(dp, 4)
        z, l, c = ex // 4, (ex // 2) % 2, ex % 2
        j_dp = ((h + dh) % 2) * 4 + (y + dy) % 4
        j_ex = ((z + dz) % 4) * 4 + ((l + dl) % 2) * 2 + (c + dc) % 2
        pairs.append((i, j_dp * 16 + j_ex))
    return lax.ppermute(x, AXES, pairs)


def dot(a, b, ca=1, cb=0):
    return lax.dot_general(a, b, (((ca,), (cb,)), ((), ())), preferred_element_type=F32)


def total(*parts, dtype=BF):
    out = parts[0].astype(F32)
    for part in parts[1:]:
        out = out + part.astype(F32)
    return out.astype(dtype)


VMEM = pl.BlockSpec(memory_space=pltpu.VMEM)
SMEM = pl.BlockSpec(memory_space=pltpu.SMEM)
AFTER = pl.BlockSpec(memory_space=pl.ANY)


def call(kernel, name, outs, args, scratch=(), in_specs=None, out_specs=None):
    return pl.pallas_call(
        kernel,
        out_shape=outs,
        in_specs=in_specs or [VMEM] * len(args),
        out_specs=out_specs or (VMEM,) * len(outs),
        scratch_shapes=list(scratch),
        compiler_params=pltpu.CompilerParams(vmem_limit_bytes=48 * 2**20),
        cost_estimate=pl.CostEstimate(flops=10**6, bytes_accessed=10**5, transcendentals=0),
        name=name,
    )(*args)


def shape(*dims, dtype=BF):
    return jax.ShapeDtypeStruct(dims, dtype)


def sum_kernel(count, *refs):
    out = refs[0][...].astype(F32)
    for ref in refs[1:count]:
        out = out + ref[...].astype(F32)
    refs[-1][...] = out.astype(BF)


def stack_kernel(*refs):
    for k in range(4):
        refs[-1][k] = refs[k][...]


def sum_after(parts, after, name):
    return call(
        functools.partial(sum_kernel, len(parts)),
        name,
        (shape(*parts[0].shape),),
        (*parts, *after),
        in_specs=[VMEM] * len(parts) + [AFTER] * len(after),
    )[0]


def select(pos, gates, rows, shift):
    row = lax.broadcasted_iota(jnp.int32, (rows, 256), 0) + shift
    m0 = row == pos[0:1, :]
    m1 = row == pos[1:2, :]
    pick = jnp.where(m0 | m1, 1.0, 0.0).astype(BF)
    gate = jnp.where(m0, gates[0:1, :], 0.0) + jnp.where(m1, gates[1:2, :], 0.0)
    return pick, jnp.sum(gate, axis=1, keepdims=True)


def route_kernel(
    here_ref, ids_ref, dest_ref, slot_ref, gate_ref, tok_ref, cot_ref, in_ref, out_ref, pick_ref,
    parts_ref, hot_ref, pos_ref, top_ref,
):
    l, c = here_ref[3], here_ref[4]
    pick = pick_ref[...]
    gate_w = dot(pick, in_ref[:, :768], 0, 1).astype(BF)
    up_w = dot(pick, in_ref[:, 768:], 0, 1).astype(BF)
    down_w = dot(pick, out_ref[...], 0, 0).astype(BF)
    for q in range(4):
        units = slice(192 * q, 192 * q + 192)
        rows = jnp.concatenate([gate_w[units], up_w[units], down_w[units]], axis=0)
        parts_ref[(q // 2 + c) % 2, (q % 2 + l) % 2] = rows

    ids, dest, slot = ids_ref[...], dest_ref[...], slot_ref[...]
    served = slot >= 0
    replica = served & (ids != dest)
    top_ref[0, 0] = jnp.max(jnp.where(replica, ids, -1))
    order = jnp.zeros_like(dest)
    for e in range(15):
        found = jnp.where(replica & (dest == e), 1, 0)
        found = jnp.max(jnp.max(found, axis=1, keepdims=True), axis=0, keepdims=True)
        order = order + jnp.where(dest > e, found, 0)
    pos = jnp.where(replica, 640 + order * 20 + slot, dest * 40 + slot)
    pos = jnp.where(served, pos, -1000)
    pos_ref[...] = pos
    hot_x, hot_gate = select(pos, gate_ref[...], 80, 640)
    for j in range(4):
        cols = pl.ds(j * 512, 512)
        hot_ref[0:80, cols] = dot(hot_x, tok_ref[:, cols]).astype(BF)
        hot_ref[80:160, cols] = (hot_gate * dot(hot_x, cot_ref[:, cols])).astype(BF)


def route(here, tables, rows, weights, pick):
    i32 = jnp.int32
    whole = lambda *dims: pl.BlockSpec(dims, lambda i, d: (0,) * len(dims))
    return pl.pallas_call(
        route_kernel,
        out_shape=(
            shape(2, 2, 576, 256),
            shape(160, 2048),
            shape(2, 256, dtype=i32),
            shape(1, 1, dtype=i32),
        ),
        grid_spec=pltpu.PrefetchScalarGridSpec(
            num_scalar_prefetch=1,
            grid=(1,),
            in_specs=[whole(2, 256)] * 4
            + [whole(256, 2048)] * 2
            + [
                pl.BlockSpec((256, 1536), lambda i, d: (d[0] * 4 + d[1], 0)),
                pl.BlockSpec((768, 256), lambda i, d: (0, d[0] * 4 + d[1])),
                whole(768, 768),
            ],
            out_specs=(whole(2, 2, 576, 256), whole(160, 2048), whole(2, 256), SMEM),
        ),
        compiler_params=pltpu.CompilerParams(vmem_limit_bytes=40 * 2**20),
        cost_estimate=pl.CostEstimate(flops=10**6, bytes_accessed=10**5, transcendentals=0),
        name="route",
    )(here, *tables, *rows, *weights, pick)


def pack_kernel(pos_ref, gate_ref, tok_ref, cot_ref, *refs):
    send_ref = refs[-1]
    home_x, _ = select(pos_ref[...], gate_ref[...], 640, 0)
    home_g, home_gate = select(pos_ref[...], gate_ref[...], 640, -20)
    for j in range(4):
        cols = pl.ds(j * 512, 512)
        rows = dot(home_x, tok_ref[:, cols]) + home_gate * dot(home_g, cot_ref[:, cols])
        send_ref[:, cols] = rows.astype(BF)


def unpack_kernel(pos_ref, gate_ref, ret_ref, hot_a_ref, hot_b_ref, mixed_ref, grad_ref):
    def select(k, rows, shift):
        row = lax.broadcasted_iota(jnp.int32, (rows, 256), 0) + shift
        return jnp.where(row == pos_ref[k : k + 1, :], 1.0, 0.0).astype(BF)

    out0, out1 = select(0, 640, 0), select(1, 640, 0)
    back = select(0, 640, -20) + select(1, 640, -20)
    hot0, hot1 = select(0, 80, 640), select(1, 80, 640)
    hot_back = hot0 + hot1
    gate0, gate1 = gate_ref[:, 0:1], gate_ref[:, 1:2]
    for j in range(4):
        cols = pl.ds(j * 512, 512)
        ret = ret_ref[:, cols]
        hot = (hot_a_ref[0, :, cols].astype(F32) + hot_b_ref[:, cols].astype(F32)).astype(BF)
        first = dot(out0, ret, 0, 0) + dot(hot0, hot[:80], 0, 0)
        second = dot(out1, ret, 0, 0) + dot(hot1, hot[:80], 0, 0)
        mixed_ref[:, cols] = (gate0 * first + gate1 * second).astype(BF)
        grads = dot(back, ret, 0, 0) + dot(hot_back, hot[80:], 0, 0)
        grad_ref[:, cols] = grads.astype(BF)


def swiglu(gate, up, grad_active):
    sig = 1.0 / (1.0 + jnp.exp(-gate))
    silu = gate * sig
    active = silu * up
    grad_gate = grad_active * up * sig * (1.0 + gate * (1.0 - sig))
    return active.astype(BF), grad_gate.astype(BF), (grad_active * silu).astype(BF)


def home_kernel(
    recv_ref, pick_x_ref, pick_g_ref, in_ref, out_ref, after_ref, act_ref, gh_ref, x_ref, g_ref
):
    for k in range(4):
        recv = recv_ref[160 * k : 160 * k + 160, :]
        x_ref[80 * k : 80 * k + 80, :] = dot(pick_x_ref[...], recv).astype(BF)
        g_ref[80 * k : 80 * k + 80, :] = dot(pick_g_ref[...], recv).astype(BF)

    def unit_tile(n, carry):
        lo = pl.ds(pl.multiple_of(n * 256, 256), 256)
        hi = pl.ds(pl.multiple_of(768 + n * 256, 256), 256)
        gate = dot(x_ref[...], in_ref[:, lo])
        up = dot(x_ref[...], in_ref[:, hi])
        grad_active = dot(g_ref[...], out_ref[lo, :], 1, 1)
        active, grad_gate, grad_up = swiglu(gate, up, grad_active)
        act_ref[:, lo] = active
        gh_ref[:, lo] = grad_gate
        gh_ref[:, hi] = grad_up
        return carry

    lax.fori_loop(0, 3, unit_tile, 0)


def grads_kernel(here_ref, act_ref, gh_ref, x_ref, g_ref, *refs):
    own_ref, up_ref, dn_ref, to_up_ref, to_dn_ref, out_own_ref, out_far_ref = refs[-7:]
    h, y = here_ref[0], here_ref[1]
    pieces = (
        (own_ref, own_ref),
        (up_ref, to_up_ref.at[1]),
        (to_up_ref.at[0], to_dn_ref.at[1]),
        (to_dn_ref.at[0], dn_ref),
    )

    def side(r, carry):
        hh = h + r - 2 * h * r
        for s, (first, second) in enumerate(pieces):
            block = hh * 4 + (y + s) % 4
            rows = x_ref[:, pl.ds(pl.multiple_of(block * 256, 256), 256)]
            grad = dot(rows, gh_ref[...], 0, 0).astype(BF)
            if s == 0:
                own_ref[r] = grad
            else:
                first[r] = grad[:, :768]
                second[r] = grad[:, 768:]
        return carry

    lax.fori_loop(0, 2, side, 0)
    for r, dst in enumerate((out_own_ref, out_far_ref)):
        hh = h if r == 0 else 1 - h
        units = act_ref[:, pl.ds(pl.multiple_of(hh * 384, 128), 384)]
        for j in range(4):
            cols = pl.ds(j * 512, 512)
            grad = dot(units, g_ref[:, cols], 0, 0).astype(BF)
            for k in range(4):
                dst[(k + 4 - y) % 4, :, cols] = grad[96 * k : 96 * k + 96]


def result_kernel(
    act_ref, gh_ref, pick_x_ref, pick_g_ref, in_ref, out_ref, after_ref, res_ref
):
    def tile(j, carry):
        cols = pl.ds(pl.multiple_of(j * 512, 512), 512)
        out = dot(act_ref[...], out_ref[:, cols]).astype(BF)
        back = dot(gh_ref[...], in_ref[cols, :], 1, 1).astype(BF)
        both_rows = dot(pick_x_ref[...], out, 0, 0) + dot(pick_g_ref[...], back, 0, 0)
        res_ref[:, cols] = both_rows.astype(BF)
        return carry

    lax.fori_loop(0, 4, tile, 0)


def hot_kernel(
    here_ref, own_ref, near_ref, far_ref, w0_ref, w1_ref, w2_ref, w3_ref, after_ref,
    mine_ref, theirs_ref, p0_ref, p1_ref, p2_ref, p3_ref, x_ref, g_ref, t_ref,
):
    h, y, z = here_ref[0], here_ref[1], here_ref[2]
    for k, rows in enumerate((own_ref, near_ref, far_ref.at[0], far_ref.at[1])):
        x_ref[80 * k : 80 * k + 80, :] = rows[0:80, :]
        g_ref[80 * k : 80 * k + 80, :] = rows[80:160, :]
    blocks = []
    for s, w in enumerate((w0_ref, w1_ref, w2_ref, w3_ref)):
        for r in range(2):
            d = (h if r == 0 else 1 - h) * 4 + (y + 4 - s) % 4
            blocks.append((d, pl.ds(pl.multiple_of(d * 256, 256), 256), w.at[r]))
    hidden = jnp.zeros((320, 384), F32)
    grad_active = jnp.zeros((320, 192), F32)
    for d, cols, w in blocks:
        hidden = hidden + dot(x_ref[:, cols], w[0:384, :], 1, 1)
        grad_active = grad_active + dot(g_ref[:, cols], w[384:576, :], 1, 1)
    active, grad_gate, grad_up = swiglu(hidden[:, :192], hidden[:, 192:], grad_active)
    grad_hidden = jnp.concatenate([grad_gate, grad_up], axis=1)
    for b in range(8):
        down = dot(active, g_ref[:, 256 * b : 256 * b + 256], 0, 0).astype(BF)
        for d in range(8):
            t_ref[d, 384 + 24 * b : 408 + 24 * b, :] = down[24 * d : 24 * d + 24, :]
    for d, cols, w in blocks:
        t_ref[d, 0:384, :] = dot(grad_hidden, x_ref[:, cols], 0, 0).astype(BF)
        out = dot(active, w[384:576, :]).astype(BF)
        back = dot(grad_hidden, w[0:384, :]).astype(BF)
        for k, dst in enumerate((mine_ref.at[0], mine_ref.at[1], theirs_ref.at[0], theirs_ref.at[1])):
            dst[0:80, cols] = out[80 * k : 80 * k + 80]
            dst[80:160, cols] = back[80 * k : 80 * k + 80]
    for n, p in enumerate((p0_ref, p1_ref, p2_ref, p3_ref)):
        rows = pl.ds(pl.multiple_of((z + n) % 4 * 144, 16), 144)
        for s in range(4):
            for r in range(2):
                p[r, s] = t_ref[(h if r == 0 else 1 - h) * 4 + (y + s) % 4, rows, :]


def finish_kernel(
    here_ref, spare_ref, more_ref, pick_ref, in_ref, in_got_ref, d0_ref, d1_ref, d2_ref, d3_ref,
    after_ref, out_in_ref, out_down_ref, t_ref,
):
    z, l, c = here_ref[2], here_ref[3], here_ref[4]
    flag = here_ref[5].astype(F32)
    for rc, src in enumerate((spare_ref, more_ref)):
        for rl in range(2):
            q = 2 * (c if rc == 0 else 1 - c) + (l if rl == 0 else 1 - l)
            for s in range(4):
                rows = pl.ds(pl.multiple_of((z + 4 - s) % 4 * 144, 16), 144)
                t_ref[q, rows, :] = src[rl, s]
    pick = pick_ref[...]
    for part in range(2):
        rows = jnp.concatenate(
            [t_ref[q, 192 * part : 192 * part + 192, :] for q in range(4)], axis=0
        )
        cols = slice(768 * part, 768 * part + 768)
        home = in_ref[:, cols].astype(F32) + in_got_ref[:, cols].astype(F32)
        out_in_ref[:, cols] = home + flag * dot(rows, pick, 0, 1)
    for q in range(4):
        for b in range(8):
            rows, cols = slice(24 * q, 24 * q + 24), slice(256 * b, 256 * b + 256)
            home = d0_ref[rows, cols].astype(F32) + d1_ref[rows, cols].astype(F32)
            home = home + d2_ref[rows, cols].astype(F32) + d3_ref[rows, cols].astype(F32)
            piece = t_ref[q, 384 + 24 * b : 408 + 24 * b, :].astype(F32)
            out_down_ref[rows, cols] = home + flag * piece


def shards(tokens, cotangent, route_gates, w_gate_up, w_down, expert_ids, dest_ranks, slot_ids):
    dp, ex = lax.axis_index("dp"), lax.axis_index("expert")
    h, y = dp // 4, dp % 4
    z, l, c = ex // 4, (ex // 2) % 2, ex % 2
    w_in, w_out = w_gate_up[0], w_down[0]
    i32 = jnp.int32

    unit = jnp.arange(768, dtype=i32)
    place = unit % 192 // 24 * 96 + unit // 192 * 24 + unit % 24
    pick = (unit[:, None] == place[None, :]).astype(BF)
    here = jnp.stack([h, y, z, l, c]).astype(i32)
    tables = (expert_ids.T, dest_ranks.T, slot_ids.T, route_gates.T)
    parts, hot_rows, pos, hot = route(here, tables, (tokens, cotangent), (w_in, w_out), pick)
    hot = hot[0, 0]
    hz, hl, hc = hot // 4, (hot // 2) % 2, hot % 2
    here = jnp.concatenate([here, (ex == hot).astype(i32).reshape(1)])

    got = hop(parts[1], dc=1)
    piece = jnp.where(c == hc, parts[0], got)
    near_w = hop(piece[1], dl=1)
    piece = jnp.where(l == hl, piece[0], near_w)
    got = [hop(piece, dz=s) for s in (1, 2, 3)]
    away = (z - hz) % 4
    piece = jnp.where(
        away == 0, piece, jnp.where(away == 1, got[0], jnp.where(away == 2, got[1], got[2]))
    )
    hot_rows = sum_after([hot_rows], [near_w], "keep_rows")
    near_rows = hop(hot_rows, dl=1)
    far_rows = hop(jnp.stack([hot_rows, near_rows]), dc=1)
    piece = jnp.stack([piece, hop(piece, dh=1)])

    (send,) = call(
        pack_kernel,
        "pack_rows",
        (shape(640, 2048),),
        (pos, tables[3], tokens, cotangent, piece, near_rows),
        in_specs=[VMEM] * 4 + [AFTER] * 2,
    )
    recv = lax.all_to_all(send, "expert", split_axis=0, concat_axis=0, tiled=True)
    hot_w = [piece] + [hop(piece, dy=s) for s in (1, 2, 3)]

    mine, theirs, *spares = call(
        hot_kernel,
        "hot_expert",
        (shape(2, 160, 2048), shape(2, 160, 2048)) + (shape(2, 4, 144, 256),) * 4,
        (here, hot_rows, near_rows, far_rows, *hot_w, recv),
        scratch=(
            pltpu.VMEM((320, 2048), BF),
            pltpu.VMEM((320, 2048), BF),
            pltpu.VMEM((8, 576, 256), BF),
        ),
        in_specs=[SMEM] + [VMEM] * 7 + [AFTER],
    )
    mine = total(mine, hop(theirs, dc=1))
    near_part = hop(mine[1], dl=1)

    def picks(rows, stride):
        compact = jnp.arange(rows, dtype=i32)
        spread = compact // 20 * stride + compact % 20
        row = jnp.arange(rows // 20 * stride, dtype=i32)
        return [(spread[:, None] + shift == row).astype(BF) for shift in (0, 20)]

    pick_x, pick_g = picks(80, 40)
    back_x, back_g = picks(320, 40)
    active, grad_hidden, rows_x, rows_g = call(
        home_kernel,
        "home_hidden",
        (shape(320, 768), shape(320, 1536), shape(320, 2048), shape(320, 2048)),
        (recv, pick_x, pick_g, w_in, w_out, spares[0]),
        in_specs=[VMEM] * 5 + [AFTER],
    )
    (result,) = call(
        result_kernel,
        "home_rows",
        (shape(640, 2048),),
        (active, grad_hidden, back_x, back_g, w_in, w_out, near_part),
        in_specs=[VMEM] * 6 + [AFTER],
    )
    returned = lax.all_to_all(result, "expert", split_axis=0, concat_axis=0, tiled=True)
    spare = sum_after(
        [spares[0]] + [hop(spares[s], dz=s) for s in (1, 2, 3)], [result], "sum_z"
    )
    spare = total(spare[0], hop(spare[1], dh=1))
    spare = total(spare[0], *[hop(spare[s], dy=s) for s in (1, 2, 3)])
    half = shape(2, 256, 768)
    in_own, up_a, dn_b, to_up, to_dn, out_own, out_far = call(
        grads_kernel,
        "home_grads",
        (shape(2, 256, 1536),) + (half,) * 2 + (shape(2, 2, 256, 768),) * 2 + (shape(4, 96, 2048),) * 2,
        (here, active, grad_hidden, rows_x, rows_g, spare),
        in_specs=[SMEM] + [VMEM] * 4 + [AFTER],
    )

    from_dn, from_up = hop(to_up, dy=1), hop(to_dn, dy=3)
    out_far = hop(out_far, dh=1)
    mixed, token_grad = call(
        unpack_kernel,
        "unpack_rows",
        (shape(256, 2048), shape(256, 2048)),
        (pos, route_gates, returned, mine, near_part),
    )

    (spare,) = call(
        stack_kernel,
        "stack_z",
        (shape(4, 144, 256),),
        (spare, *[hop(spare, dz=s) for s in (1, 2, 3)]),
        in_specs=[VMEM] * 4,
    )
    spare = jnp.stack([spare, hop(spare, dl=1)])
    more = hop(spare, dc=1)
    up_a = hop(sum_after([up_a, from_dn[0]], [returned], "sum_up"), dy=1)
    dn_b = hop(sum_after([dn_b, from_up[1]], [returned], "sum_down"), dy=3)
    up_b, dn_a = from_dn[1], from_up[0]
    in_sum = total(
        in_own, jnp.concatenate([up_a, up_b], axis=2), jnp.concatenate([dn_a, dn_b], axis=2)
    )
    in_got = hop(in_sum[1], dh=1)
    out_sum = total(out_own, out_far)
    out_parts = [out_sum[0]] + [hop(out_sum[s], dy=s) for s in (1, 2, 3)]

    grad_gate_up, grad_down = call(
        finish_kernel,
        "finish_grads",
        (shape(256, 1536, dtype=F32), shape(96, 2048, dtype=F32)),
        (here, spare, more, pick, in_sum[0], in_got, *out_parts, mixed),
        scratch=(pltpu.VMEM((4, 576, 256), BF),),
        in_specs=[SMEM] + [VMEM] * 9 + [AFTER],
    )
    return mixed, token_grad, grad_gate_up[None], grad_down[None]


def solution(mesh):
    rows = P(AXES, None)
    weights = P("expert", None, None)
    grads = P("expert", "dp", None)
    return jax.shard_map(
        shards,
        mesh=mesh,
        in_specs=(rows, rows, rows, weights, weights, rows, rows, rows),
        out_specs=(rows, rows, grads, grads),
        check_vma=False,
    )
```

```python
import functools

import jax
import jax.numpy as jnp
from jax import lax
from jax.experimental import pallas as pl
from jax.experimental.pallas import tpu as pltpu
from jax.sharding import PartitionSpec as P

AXES = ("dp", "expert")
BF = jnp.bfloat16
F32 = jnp.float32


def hop(x, dh=0, dy=0, dz=0, dl=0, dc=0):
    pairs = []
    for i in range(128):
        dp, ex = divmod(i, 16)
        h, y = divmod(dp, 4)
        z, l, c = ex // 4, (ex // 2) % 2, ex % 2
        j_dp = ((h + dh) % 2) * 4 + (y + dy) % 4
        j_ex = ((z + dz) % 4) * 4 + ((l + dl) % 2) * 2 + (c + dc) % 2
        pairs.append((i, j_dp * 16 + j_ex))
    return lax.ppermute(x, AXES, pairs)


def dot(a, b, ca=1, cb=0):
    return lax.dot_general(a, b, (((ca,), (cb,)), ((), ())), preferred_element_type=F32)


def total(*parts, dtype=BF):
    out = parts[0].astype(F32)
    for part in parts[1:]:
        out = out + part.astype(F32)
    return out.astype(dtype)


VMEM = pl.BlockSpec(memory_space=pltpu.VMEM)
SMEM = pl.BlockSpec(memory_space=pltpu.SMEM)
AFTER = pl.BlockSpec(memory_space=pl.ANY)


def call(kernel, name, outs, args, scratch=(), in_specs=None, out_specs=None):
    return pl.pallas_call(
        kernel,
        out_shape=outs,
        in_specs=in_specs or [VMEM] * len(args),
        out_specs=out_specs or (VMEM,) * len(outs),
        scratch_shapes=list(scratch),
        compiler_params=pltpu.CompilerParams(vmem_limit_bytes=48 * 2**20),
        cost_estimate=pl.CostEstimate(flops=10**6, bytes_accessed=10**5, transcendentals=0),
        name=name,
    )(*args)


def shape(*dims, dtype=BF):
    return jax.ShapeDtypeStruct(dims, dtype)


def sum_kernel(count, *refs):
    out = refs[0][...].astype(F32)
    for ref in refs[1:count]:
        out = out + ref[...].astype(F32)
    refs[-1][...] = out.astype(BF)


def stack_kernel(*refs):
    for k in range(4):
        refs[-1][k] = refs[k][...]


def sum_after(parts, after, name):
    return call(
        functools.partial(sum_kernel, len(parts)),
        name,
        (shape(*parts[0].shape),),
        (*parts, *after),
        in_specs=[VMEM] * len(parts) + [AFTER] * len(after),
    )[0]


def select(pos, gates, rows, shift):
    row = lax.broadcasted_iota(jnp.int32, (rows, 256), 0) + shift
    m0 = row == pos[0:1, :]
    m1 = row == pos[1:2, :]
    pick = jnp.where(m0 | m1, 1.0, 0.0).astype(BF)
    gate = jnp.where(m0, gates[0:1, :], 0.0) + jnp.where(m1, gates[1:2, :], 0.0)
    return pick, jnp.sum(gate, axis=1, keepdims=True)


def route_kernel(
    here_ref, ids_ref, dest_ref, slot_ref, gate_ref, tok_ref, cot_ref, in_ref, out_ref, pick_ref,
    parts_ref, hot_ref, pos_ref, top_ref,
):
    l, c = here_ref[3], here_ref[4]
    pick = pick_ref[...]
    gate_w = dot(pick, in_ref[:, :768], 0, 1).astype(BF)
    up_w = dot(pick, in_ref[:, 768:], 0, 1).astype(BF)
    down_w = dot(pick, out_ref[...], 0, 0).astype(BF)
    for q in range(4):
        units = slice(192 * q, 192 * q + 192)
        rows = jnp.concatenate([gate_w[units], up_w[units], down_w[units]], axis=0)
        parts_ref[(q // 2 + c) % 2, (q % 2 + l) % 2] = rows

    ids, dest, slot = ids_ref[...], dest_ref[...], slot_ref[...]
    served = slot >= 0
    replica = served & (ids != dest)
    top_ref[0, 0] = jnp.max(jnp.where(replica, ids, -1))
    order = jnp.zeros_like(dest)
    for e in range(15):
        found = jnp.where(replica & (dest == e), 1, 0)
        found = jnp.max(jnp.max(found, axis=1, keepdims=True), axis=0, keepdims=True)
        order = order + jnp.where(dest > e, found, 0)
    pos = jnp.where(replica, 640 + order * 20 + slot, dest * 40 + slot)
    pos = jnp.where(served, pos, -1000)
    pos_ref[...] = pos
    hot_x, hot_gate = select(pos, gate_ref[...], 80, 640)
    for j in range(4):
        cols = pl.ds(j * 512, 512)
        hot_ref[0:80, cols] = dot(hot_x, tok_ref[:, cols]).astype(BF)
        hot_ref[80:160, cols] = (hot_gate * dot(hot_x, cot_ref[:, cols])).astype(BF)


def route(here, tables, rows, weights, pick):
    i32 = jnp.int32
    whole = lambda *dims: pl.BlockSpec(dims, lambda i, d: (0,) * len(dims))
    return pl.pallas_call(
        route_kernel,
        out_shape=(
            shape(2, 2, 576, 256),
            shape(160, 2048),
            shape(2, 256, dtype=i32),
            shape(1, 1, dtype=i32),
        ),
        grid_spec=pltpu.PrefetchScalarGridSpec(
            num_scalar_prefetch=1,
            grid=(1,),
            in_specs=[whole(2, 256)] * 4
            + [whole(256, 2048)] * 2
            + [
                pl.BlockSpec((256, 1536), lambda i, d: (d[0] * 4 + d[1], 0)),
                pl.BlockSpec((768, 256), lambda i, d: (0, d[0] * 4 + d[1])),
                whole(768, 768),
            ],
            out_specs=(whole(2, 2, 576, 256), whole(160, 2048), whole(2, 256), SMEM),
        ),
        compiler_params=pltpu.CompilerParams(vmem_limit_bytes=40 * 2**20),
        cost_estimate=pl.CostEstimate(flops=10**6, bytes_accessed=10**5, transcendentals=0),
        name="route",
    )(here, *tables, *rows, *weights, pick)


def pack_kernel(pos_ref, gate_ref, tok_ref, cot_ref, *refs):
    send_ref = refs[-1]
    home_x, _ = select(pos_ref[...], gate_ref[...], 640, 0)
    home_g, home_gate = select(pos_ref[...], gate_ref[...], 640, -20)
    for j in range(4):
        cols = pl.ds(j * 512, 512)
        rows = dot(home_x, tok_ref[:, cols]) + home_gate * dot(home_g, cot_ref[:, cols])
        send_ref[:, cols] = rows.astype(BF)


def unpack_kernel(pos_ref, gate_ref, ret_ref, hot_a_ref, hot_b_ref, mixed_ref, grad_ref):
    def select(k, rows, shift):
        row = lax.broadcasted_iota(jnp.int32, (rows, 256), 0) + shift
        return jnp.where(row == pos_ref[k : k + 1, :], 1.0, 0.0).astype(BF)

    out0, out1 = select(0, 640, 0), select(1, 640, 0)
    back = select(0, 640, -20) + select(1, 640, -20)
    hot0, hot1 = select(0, 80, 640), select(1, 80, 640)
    hot_back = hot0 + hot1
    gate0, gate1 = gate_ref[:, 0:1], gate_ref[:, 1:2]
    for j in range(4):
        cols = pl.ds(j * 512, 512)
        ret = ret_ref[:, cols]
        hot = (hot_a_ref[0, :, cols].astype(F32) + hot_b_ref[:, cols].astype(F32)).astype(BF)
        first = dot(out0, ret, 0, 0) + dot(hot0, hot[:80], 0, 0)
        second = dot(out1, ret, 0, 0) + dot(hot1, hot[:80], 0, 0)
        mixed_ref[:, cols] = (gate0 * first + gate1 * second).astype(BF)
        grads = dot(back, ret, 0, 0) + dot(hot_back, hot[80:], 0, 0)
        grad_ref[:, cols] = grads.astype(BF)


def swiglu(gate, up, grad_active):
    sig = 1.0 / (1.0 + jnp.exp(-gate))
    silu = gate * sig
    active = silu * up
    grad_gate = grad_active * up * sig * (1.0 + gate * (1.0 - sig))
    return active.astype(BF), grad_gate.astype(BF), (grad_active * silu).astype(BF)


def home_kernel(
    recv_ref, pick_x_ref, pick_g_ref, in_ref, out_ref, after_ref, act_ref, gh_ref, x_ref, g_ref
):
    for k in range(4):
        recv = recv_ref[160 * k : 160 * k + 160, :]
        x_ref[80 * k : 80 * k + 80, :] = dot(pick_x_ref[...], recv).astype(BF)
        g_ref[80 * k : 80 * k + 80, :] = dot(pick_g_ref[...], recv).astype(BF)

    def unit_tile(n, carry):
        lo = pl.ds(pl.multiple_of(n * 256, 256), 256)
        hi = pl.ds(pl.multiple_of(768 + n * 256, 256), 256)
        gate = dot(x_ref[...], in_ref[:, lo])
        up = dot(x_ref[...], in_ref[:, hi])
        grad_active = dot(g_ref[...], out_ref[lo, :], 1, 1)
        active, grad_gate, grad_up = swiglu(gate, up, grad_active)
        act_ref[:, lo] = active
        gh_ref[:, lo] = grad_gate
        gh_ref[:, hi] = grad_up
        return carry

    lax.fori_loop(0, 3, unit_tile, 0)


def grads_kernel(here_ref, act_ref, gh_ref, x_ref, g_ref, *refs):
    own_ref, up_ref, dn_ref, to_up_ref, to_dn_ref, out_own_ref, out_far_ref = refs[-7:]
    h, y = here_ref[0], here_ref[1]
    pieces = (
        (own_ref, own_ref),
        (up_ref, to_up_ref.at[1]),
        (to_up_ref.at[0], to_dn_ref.at[1]),
        (to_dn_ref.at[0], dn_ref),
    )

    def side(r, carry):
        hh = h + r - 2 * h * r
        for s, (first, second) in enumerate(pieces):
            block = hh * 4 + (y + s) % 4
            rows = x_ref[:, pl.ds(pl.multiple_of(block * 256, 256), 256)]
            grad = dot(rows, gh_ref[...], 0, 0).astype(BF)
            if s == 0:
                own_ref[r] = grad
            else:
                first[r] = grad[:, :768]
                second[r] = grad[:, 768:]
        return carry

    lax.fori_loop(0, 2, side, 0)
    for r, dst in enumerate((out_own_ref, out_far_ref)):
        hh = h if r == 0 else 1 - h
        units = act_ref[:, pl.ds(pl.multiple_of(hh * 384, 128), 384)]
        for j in range(4):
            cols = pl.ds(j * 512, 512)
            grad = dot(units, g_ref[:, cols], 0, 0).astype(BF)
            for k in range(4):
                dst[(k + 4 - y) % 4, :, cols] = grad[96 * k : 96 * k + 96]


def result_kernel(
    act_ref, gh_ref, pick_x_ref, pick_g_ref, in_ref, out_ref, after_ref, res_ref
):
    def tile(j, carry):
        cols = pl.ds(pl.multiple_of(j * 512, 512), 512)
        out = dot(act_ref[...], out_ref[:, cols]).astype(BF)
        back = dot(gh_ref[...], in_ref[cols, :], 1, 1).astype(BF)
        both_rows = dot(pick_x_ref[...], out, 0, 0) + dot(pick_g_ref[...], back, 0, 0)
        res_ref[:, cols] = both_rows.astype(BF)
        return carry

    lax.fori_loop(0, 4, tile, 0)


def hot_kernel(
    here_ref, own_ref, near_ref, far_ref, w0_ref, w1_ref, w2_ref, w3_ref, after_ref,
    mine_ref, theirs_ref, p0_ref, p1_ref, p2_ref, p3_ref, x_ref, g_ref, t_ref,
):
    h, y, z = here_ref[0], here_ref[1], here_ref[2]
    for k, rows in enumerate((own_ref, near_ref, far_ref.at[0], far_ref.at[1])):
        x_ref[80 * k : 80 * k + 80, :] = rows[0:80, :]
        g_ref[80 * k : 80 * k + 80, :] = rows[80:160, :]
    blocks = []
    for s, w in enumerate((w0_ref, w1_ref, w2_ref, w3_ref)):
        for r in range(2):
            d = (h if r == 0 else 1 - h) * 4 + (y + 4 - s) % 4
            blocks.append((d, pl.ds(pl.multiple_of(d * 256, 256), 256), w.at[r]))
    hidden = jnp.zeros((320, 384), F32)
    grad_active = jnp.zeros((320, 192), F32)
    for d, cols, w in blocks:
        hidden = hidden + dot(x_ref[:, cols], w[0:384, :], 1, 1)
        grad_active = grad_active + dot(g_ref[:, cols], w[384:576, :], 1, 1)
    active, grad_gate, grad_up = swiglu(hidden[:, :192], hidden[:, 192:], grad_active)
    grad_hidden = jnp.concatenate([grad_gate, grad_up], axis=1)
    for b in range(8):
        down = dot(active, g_ref[:, 256 * b : 256 * b + 256], 0, 0).astype(BF)
        for d in range(8):
            t_ref[d, 384 + 24 * b : 408 + 24 * b, :] = down[24 * d : 24 * d + 24, :]
    for d, cols, w in blocks:
        t_ref[d, 0:384, :] = dot(grad_hidden, x_ref[:, cols], 0, 0).astype(BF)
        out = dot(active, w[384:576, :]).astype(BF)
        back = dot(grad_hidden, w[0:384, :]).astype(BF)
        for k, dst in enumerate((mine_ref.at[0], mine_ref.at[1], theirs_ref.at[0], theirs_ref.at[1])):
            dst[0:80, cols] = out[80 * k : 80 * k + 80]
            dst[80:160, cols] = back[80 * k : 80 * k + 80]
    for n, p in enumerate((p0_ref, p1_ref, p2_ref, p3_ref)):
        rows = pl.ds(pl.multiple_of((z + n) % 4 * 144, 16), 144)
        for s in range(4):
            for r in range(2):
                p[r, s] = t_ref[(h if r == 0 else 1 - h) * 4 + (y + s) % 4, rows, :]


def finish_kernel(
    here_ref, spare_ref, more_ref, pick_ref, in_ref, in_got_ref, d0_ref, d1_ref, d2_ref, d3_ref,
    after_ref, out_in_ref, out_down_ref, t_ref,
):
    z, l, c = here_ref[2], here_ref[3], here_ref[4]
    flag = here_ref[5].astype(F32)
    for rc, src in enumerate((spare_ref, more_ref)):
        for rl in range(2):
            q = 2 * (c if rc == 0 else 1 - c) + (l if rl == 0 else 1 - l)
            for s in range(4):
                rows = pl.ds(pl.multiple_of((z + 4 - s) % 4 * 144, 16), 144)
                t_ref[q, rows, :] = src[rl, s]
    pick = pick_ref[...]
    for part in range(2):
        rows = jnp.concatenate(
            [t_ref[q, 192 * part : 192 * part + 192, :] for q in range(4)], axis=0
        )
        cols = slice(768 * part, 768 * part + 768)
        home = in_ref[:, cols].astype(F32) + in_got_ref[:, cols].astype(F32)
        out_in_ref[:, cols] = home + flag * dot(rows, pick, 0, 1)
    for q in range(4):
        for b in range(8):
            rows, cols = slice(24 * q, 24 * q + 24), slice(256 * b, 256 * b + 256)
            home = d0_ref[rows, cols].astype(F32) + d1_ref[rows, cols].astype(F32)
            home = home + d2_ref[rows, cols].astype(F32) + d3_ref[rows, cols].astype(F32)
            piece = t_ref[q, 384 + 24 * b : 408 + 24 * b, :].astype(F32)
            out_down_ref[rows, cols] = home + flag * piece


def shards(tokens, cotangent, route_gates, w_gate_up, w_down, expert_ids, dest_ranks, slot_ids):
    dp, ex = lax.axis_index("dp"), lax.axis_index("expert")
    h, y = dp // 4, dp % 4
    z, l, c = ex // 4, (ex // 2) % 2, ex % 2
    w_in, w_out = w_gate_up[0], w_down[0]
    i32 = jnp.int32

    unit = jnp.arange(768, dtype=i32)
    place = unit % 192 // 24 * 96 + unit // 192 * 24 + unit % 24
    pick = (unit[:, None] == place[None, :]).astype(BF)
    here = jnp.stack([h, y, z, l, c]).astype(i32)
    tables = (expert_ids.T, dest_ranks.T, slot_ids.T, route_gates.T)
    parts, hot_rows, pos, hot = route(here, tables, (tokens, cotangent), (w_in, w_out), pick)
    hot = hot[0, 0]
    hz, hl, hc = hot // 4, (hot // 2) % 2, hot % 2
    here = jnp.concatenate([here, (ex == hot).astype(i32).reshape(1)])

    got = hop(parts[1], dc=1)
    piece = jnp.where(c == hc, parts[0], got)
    near_w = hop(piece[1], dl=1)
    piece = jnp.where(l == hl, piece[0], near_w)
    got = [hop(piece, dz=s) for s in (1, 2, 3)]
    away = (z - hz) % 4
    piece = jnp.where(
        away == 0, piece, jnp.where(away == 1, got[0], jnp.where(away == 2, got[1], got[2]))
    )
    hot_rows = sum_after([hot_rows], [near_w], "keep_rows")
    near_rows = hop(hot_rows, dl=1)
    far_rows = hop(jnp.stack([hot_rows, near_rows]), dc=1)
    piece = jnp.stack([piece, hop(piece, dh=1)])

    (send,) = call(
        pack_kernel,
        "pack_rows",
        (shape(640, 2048),),
        (pos, tables[3], tokens, cotangent, piece, near_rows),
        in_specs=[VMEM] * 4 + [AFTER] * 2,
    )
    recv = lax.all_to_all(send, "expert", split_axis=0, concat_axis=0, tiled=True)
    hot_w = [piece] + [hop(piece, dy=s) for s in (1, 2, 3)]

    mine, theirs, *spares = call(
        hot_kernel,
        "hot_expert",
        (shape(2, 160, 2048), shape(2, 160, 2048)) + (shape(2, 4, 144, 256),) * 4,
        (here, hot_rows, near_rows, far_rows, *hot_w, recv),
        scratch=(
            pltpu.VMEM((320, 2048), BF),
            pltpu.VMEM((320, 2048), BF),
            pltpu.VMEM((8, 576, 256), BF),
        ),
        in_specs=[SMEM] + [VMEM] * 7 + [AFTER],
    )
    mine = total(mine, hop(theirs, dc=1))
    near_part = hop(mine[1], dl=1)

    def picks(rows, stride):
        compact = jnp.arange(rows, dtype=i32)
        spread = compact // 20 * stride + compact % 20
        row = jnp.arange(rows // 20 * stride, dtype=i32)
        return [(spread[:, None] + shift == row).astype(BF) for shift in (0, 20)]

    pick_x, pick_g = picks(80, 40)
    back_x, back_g = picks(320, 40)
    active, grad_hidden, rows_x, rows_g = call(
        home_kernel,
        "home_hidden",
        (shape(320, 768), shape(320, 1536), shape(320, 2048), shape(320, 2048)),
        (recv, pick_x, pick_g, w_in, w_out, spares[0]),
        in_specs=[VMEM] * 5 + [AFTER],
    )
    half = shape(2, 256, 768)
    in_own, up_a, dn_b, to_up, to_dn, out_own, out_far = call(
        grads_kernel,
        "home_grads",
        (shape(2, 256, 1536),) + (half,) * 2 + (shape(2, 2, 256, 768),) * 2 + (shape(4, 96, 2048),) * 2,
        (here, active, grad_hidden, rows_x, rows_g, near_part),
        in_specs=[SMEM] + [VMEM] * 4 + [AFTER],
    )
    spare = sum_after(
        [spares[0]] + [hop(spares[s], dz=s) for s in (1, 2, 3)], [in_own], "sum_z"
    )
    (result,) = call(
        result_kernel,
        "home_rows",
        (shape(640, 2048),),
        (active, grad_hidden, back_x, back_g, w_in, w_out, spare),
        in_specs=[VMEM] * 6 + [AFTER],
    )
    returned = lax.all_to_all(result, "expert", split_axis=0, concat_axis=0, tiled=True)
    spare = total(spare[0], hop(spare[1], dh=1))
    spare = total(spare[0], *[hop(spare[s], dy=s) for s in (1, 2, 3)])

    from_dn, from_up = hop(to_up, dy=1), hop(to_dn, dy=3)
    out_sum = total(out_own, hop(out_far, dh=1))
    mixed, token_grad = call(
        unpack_kernel,
        "unpack_rows",
        (shape(256, 2048), shape(256, 2048)),
        (pos, route_gates, returned, mine, near_part),
    )

    (spare,) = call(
        stack_kernel,
        "stack_z",
        (shape(4, 144, 256),),
        (spare, *[hop(spare, dz=s) for s in (1, 2, 3)], returned, out_sum),
        in_specs=[VMEM] * 4 + [AFTER] * 2,
    )
    spare = jnp.stack([spare, hop(spare, dl=1)])
    more = hop(spare, dc=1)
    up_a = hop(sum_after([up_a, from_dn[0]], [result], "sum_up"), dy=1)
    dn_b = hop(sum_after([dn_b, from_up[1]], [result], "sum_down"), dy=3)
    up_b, dn_a = from_dn[1], from_up[0]
    in_sum = total(
        in_own, jnp.concatenate([up_a, up_b], axis=2), jnp.concatenate([dn_a, dn_b], axis=2)
    )
    in_got = hop(in_sum[1], dh=1)
    out_parts = [out_sum[0]] + [hop(out_sum[s], dy=s) for s in (1, 2, 3)]

    grad_gate_up, grad_down = call(
        finish_kernel,
        "finish_grads",
        (shape(256, 1536, dtype=F32), shape(96, 2048, dtype=F32)),
        (here, spare, more, pick, in_sum[0], in_got, *out_parts, mixed),
        scratch=(pltpu.VMEM((4, 576, 256), BF),),
        in_specs=[SMEM] + [VMEM] * 9 + [AFTER],
    )
    return mixed, token_grad, grad_gate_up[None], grad_down[None]


def solution(mesh):
    rows = P(AXES, None)
    weights = P("expert", None, None)
    grads = P("expert", "dp", None)
    return jax.shard_map(
        shards,
        mesh=mesh,
        in_specs=(rows, rows, rows, weights, weights, rows, rows, rows),
        out_specs=(rows, rows, grads, grads),
        check_vma=False,
    )
```

```python
import functools

import jax
import jax.numpy as jnp
from jax import lax
from jax.experimental import pallas as pl
from jax.experimental.pallas import tpu as pltpu
from jax.sharding import PartitionSpec as P

AXES = ("dp", "expert")
BF = jnp.bfloat16
F32 = jnp.float32


def hop(x, dh=0, dy=0, dz=0, dl=0, dc=0):
    pairs = []
    for i in range(128):
        dp, ex = divmod(i, 16)
        h, y = divmod(dp, 4)
        z, l, c = ex // 4, (ex // 2) % 2, ex % 2
        j_dp = ((h + dh) % 2) * 4 + (y + dy) % 4
        j_ex = ((z + dz) % 4) * 4 + ((l + dl) % 2) * 2 + (c + dc) % 2
        pairs.append((i, j_dp * 16 + j_ex))
    return lax.ppermute(x, AXES, pairs)


def dot(a, b, ca=1, cb=0):
    return lax.dot_general(a, b, (((ca,), (cb,)), ((), ())), preferred_element_type=F32)


def total(*parts, dtype=BF):
    out = parts[0].astype(F32)
    for part in parts[1:]:
        out = out + part.astype(F32)
    return out.astype(dtype)


VMEM = pl.BlockSpec(memory_space=pltpu.VMEM)
SMEM = pl.BlockSpec(memory_space=pltpu.SMEM)
AFTER = pl.BlockSpec(memory_space=pl.ANY)


def call(kernel, name, outs, args, scratch=(), in_specs=None, out_specs=None):
    return pl.pallas_call(
        kernel,
        out_shape=outs,
        in_specs=in_specs or [VMEM] * len(args),
        out_specs=out_specs or (VMEM,) * len(outs),
        scratch_shapes=list(scratch),
        compiler_params=pltpu.CompilerParams(vmem_limit_bytes=48 * 2**20),
        cost_estimate=pl.CostEstimate(flops=10**6, bytes_accessed=10**5, transcendentals=0),
        name=name,
    )(*args)


def shape(*dims, dtype=BF):
    return jax.ShapeDtypeStruct(dims, dtype)


def sum_kernel(count, *refs):
    out = refs[0][...].astype(F32)
    for ref in refs[1:count]:
        out = out + ref[...].astype(F32)
    refs[-1][...] = out.astype(BF)


def stack_kernel(*refs):
    for k in range(4):
        refs[-1][k] = refs[k][...]


def sum_after(parts, after, name):
    return call(
        functools.partial(sum_kernel, len(parts)),
        name,
        (shape(*parts[0].shape),),
        (*parts, *after),
        in_specs=[VMEM] * len(parts) + [AFTER] * len(after),
    )[0]


def select(pos, gates, rows, shift):
    row = lax.broadcasted_iota(jnp.int32, (rows, 256), 0) + shift
    m0 = row == pos[0:1, :]
    m1 = row == pos[1:2, :]
    pick = jnp.where(m0 | m1, 1.0, 0.0).astype(BF)
    gate = jnp.where(m0, gates[0:1, :], 0.0) + jnp.where(m1, gates[1:2, :], 0.0)
    return pick, jnp.sum(gate, axis=1, keepdims=True)


def route_kernel(
    here_ref, ids_ref, dest_ref, slot_ref, gate_ref, tok_ref, cot_ref, in_ref, out_ref, pick_ref,
    parts_ref, hot_ref, pos_ref, top_ref,
):
    l, c = here_ref[3], here_ref[4]
    pick = pick_ref[...]
    gate_w = dot(pick, in_ref[:, :768], 0, 1).astype(BF)
    up_w = dot(pick, in_ref[:, 768:], 0, 1).astype(BF)
    down_w = dot(pick, out_ref[...], 0, 0).astype(BF)
    for q in range(4):
        units = slice(192 * q, 192 * q + 192)
        rows = jnp.concatenate([gate_w[units], up_w[units], down_w[units]], axis=0)
        parts_ref[(q // 2 + c) % 2, (q % 2 + l) % 2] = rows

    ids, dest, slot = ids_ref[...], dest_ref[...], slot_ref[...]
    served = slot >= 0
    replica = served & (ids != dest)
    top_ref[0, 0] = jnp.max(jnp.where(replica, ids, -1))
    order = jnp.zeros_like(dest)
    for e in range(15):
        found = jnp.where(replica & (dest == e), 1, 0)
        found = jnp.max(jnp.max(found, axis=1, keepdims=True), axis=0, keepdims=True)
        order = order + jnp.where(dest > e, found, 0)
    pos = jnp.where(replica, 640 + order * 20 + slot, dest * 40 + slot)
    pos = jnp.where(served, pos, -1000)
    pos_ref[...] = pos
    hot_x, hot_gate = select(pos, gate_ref[...], 80, 640)
    for j in range(4):
        cols = pl.ds(j * 512, 512)
        hot_ref[0:80, cols] = dot(hot_x, tok_ref[:, cols]).astype(BF)
        hot_ref[80:160, cols] = (hot_gate * dot(hot_x, cot_ref[:, cols])).astype(BF)


def route(here, tables, rows, weights, pick):
    i32 = jnp.int32
    whole = lambda *dims: pl.BlockSpec(dims, lambda i, d: (0,) * len(dims))
    return pl.pallas_call(
        route_kernel,
        out_shape=(
            shape(2, 2, 576, 256),
            shape(160, 2048),
            shape(2, 256, dtype=i32),
            shape(1, 1, dtype=i32),
        ),
        grid_spec=pltpu.PrefetchScalarGridSpec(
            num_scalar_prefetch=1,
            grid=(1,),
            in_specs=[whole(2, 256)] * 4
            + [whole(256, 2048)] * 2
            + [
                pl.BlockSpec((256, 1536), lambda i, d: (d[0] * 4 + d[1], 0)),
                pl.BlockSpec((768, 256), lambda i, d: (0, d[0] * 4 + d[1])),
                whole(768, 768),
            ],
            out_specs=(whole(2, 2, 576, 256), whole(160, 2048), whole(2, 256), SMEM),
        ),
        compiler_params=pltpu.CompilerParams(vmem_limit_bytes=40 * 2**20),
        cost_estimate=pl.CostEstimate(flops=10**6, bytes_accessed=10**5, transcendentals=0),
        name="route",
    )(here, *tables, *rows, *weights, pick)


def pack_kernel(pos_ref, gate_ref, tok_ref, cot_ref, *refs):
    send_ref = refs[-1]
    home_x, _ = select(pos_ref[...], gate_ref[...], 640, 0)
    home_g, home_gate = select(pos_ref[...], gate_ref[...], 640, -20)
    for j in range(4):
        cols = pl.ds(j * 512, 512)
        rows = dot(home_x, tok_ref[:, cols]) + home_gate * dot(home_g, cot_ref[:, cols])
        send_ref[:, cols] = rows.astype(BF)


def unpack_kernel(pos_ref, gate_ref, ret_ref, hot_a_ref, hot_b_ref, mixed_ref, grad_ref):
    def select(k, rows, shift):
        row = lax.broadcasted_iota(jnp.int32, (rows, 256), 0) + shift
        return jnp.where(row == pos_ref[k : k + 1, :], 1.0, 0.0).astype(BF)

    out0, out1 = select(0, 640, 0), select(1, 640, 0)
    back = select(0, 640, -20) + select(1, 640, -20)
    hot0, hot1 = select(0, 80, 640), select(1, 80, 640)
    hot_back = hot0 + hot1
    gate0, gate1 = gate_ref[:, 0:1], gate_ref[:, 1:2]
    for j in range(4):
        cols = pl.ds(j * 512, 512)
        ret = ret_ref[:, cols]
        hot = (hot_a_ref[0, :, cols].astype(F32) + hot_b_ref[:, cols].astype(F32)).astype(BF)
        first = dot(out0, ret, 0, 0) + dot(hot0, hot[:80], 0, 0)
        second = dot(out1, ret, 0, 0) + dot(hot1, hot[:80], 0, 0)
        mixed_ref[:, cols] = (gate0 * first + gate1 * second).astype(BF)
        grads = dot(back, ret, 0, 0) + dot(hot_back, hot[80:], 0, 0)
        grad_ref[:, cols] = grads.astype(BF)


def swiglu(gate, up, grad_active):
    sig = 1.0 / (1.0 + jnp.exp(-gate))
    silu = gate * sig
    active = silu * up
    grad_gate = grad_active * up * sig * (1.0 + gate * (1.0 - sig))
    return active.astype(BF), grad_gate.astype(BF), (grad_active * silu).astype(BF)


def home_kernel(
    recv_ref, pick_x_ref, pick_g_ref, in_ref, out_ref, after_ref, act_ref, gh_ref, x_ref, g_ref
):
    for k in range(4):
        recv = recv_ref[160 * k : 160 * k + 160, :]
        x_ref[80 * k : 80 * k + 80, :] = dot(pick_x_ref[...], recv).astype(BF)
        g_ref[80 * k : 80 * k + 80, :] = dot(pick_g_ref[...], recv).astype(BF)

    def unit_tile(n, carry):
        lo = pl.ds(pl.multiple_of(n * 256, 256), 256)
        hi = pl.ds(pl.multiple_of(768 + n * 256, 256), 256)
        gate = dot(x_ref[...], in_ref[:, lo])
        up = dot(x_ref[...], in_ref[:, hi])
        grad_active = dot(g_ref[...], out_ref[lo, :], 1, 1)
        active, grad_gate, grad_up = swiglu(gate, up, grad_active)
        act_ref[:, lo] = active
        gh_ref[:, lo] = grad_gate
        gh_ref[:, hi] = grad_up
        return carry

    lax.fori_loop(0, 3, unit_tile, 0)


def grads_kernel(here_ref, act_ref, gh_ref, x_ref, g_ref, *refs):
    own_ref, up_ref, dn_ref, to_up_ref, to_dn_ref, out_own_ref, out_far_ref = refs[-7:]
    h, y = here_ref[0], here_ref[1]
    pieces = (
        (own_ref, own_ref),
        (up_ref, to_up_ref.at[1]),
        (to_up_ref.at[0], to_dn_ref.at[1]),
        (to_dn_ref.at[0], dn_ref),
    )

    def side(r, carry):
        hh = h + r - 2 * h * r
        for s, (first, second) in enumerate(pieces):
            block = hh * 4 + (y + s) % 4
            rows = x_ref[:, pl.ds(pl.multiple_of(block * 256, 256), 256)]
            grad = dot(rows, gh_ref[...], 0, 0).astype(BF)
            if s == 0:
                own_ref[r] = grad
            else:
                first[r] = grad[:, :768]
                second[r] = grad[:, 768:]
        return carry

    lax.fori_loop(0, 2, side, 0)
    for r, dst in enumerate((out_own_ref, out_far_ref)):
        hh = h if r == 0 else 1 - h
        units = act_ref[:, pl.ds(pl.multiple_of(hh * 384, 128), 384)]
        for j in range(4):
            cols = pl.ds(j * 512, 512)
            grad = dot(units, g_ref[:, cols], 0, 0).astype(BF)
            for k in range(4):
                dst[(k + 4 - y) % 4, :, cols] = grad[96 * k : 96 * k + 96]


def result_kernel(
    act_ref, gh_ref, pick_x_ref, pick_g_ref, in_ref, out_ref, after_ref, res_ref
):
    def tile(j, carry):
        cols = pl.ds(pl.multiple_of(j * 512, 512), 512)
        out = dot(act_ref[...], out_ref[:, cols]).astype(BF)
        back = dot(gh_ref[...], in_ref[cols, :], 1, 1).astype(BF)
        both_rows = dot(pick_x_ref[...], out, 0, 0) + dot(pick_g_ref[...], back, 0, 0)
        res_ref[:, cols] = both_rows.astype(BF)
        return carry

    lax.fori_loop(0, 4, tile, 0)


def hot_kernel(
    here_ref, own_ref, near_ref, far_ref, w0_ref, w1_ref, w2_ref, w3_ref, after_ref,
    mine_ref, theirs_ref, p0_ref, p1_ref, p2_ref, p3_ref, x_ref, g_ref, t_ref,
):
    h, y, z = here_ref[0], here_ref[1], here_ref[2]
    for k, rows in enumerate((own_ref, near_ref, far_ref.at[0], far_ref.at[1])):
        x_ref[80 * k : 80 * k + 80, :] = rows[0:80, :]
        g_ref[80 * k : 80 * k + 80, :] = rows[80:160, :]
    blocks = []
    for s, w in enumerate((w0_ref, w1_ref, w2_ref, w3_ref)):
        for r in range(2):
            d = (h if r == 0 else 1 - h) * 4 + (y + 4 - s) % 4
            blocks.append((d, pl.ds(pl.multiple_of(d * 256, 256), 256), w.at[r]))
    hidden = jnp.zeros((320, 384), F32)
    grad_active = jnp.zeros((320, 192), F32)
    for d, cols, w in blocks:
        hidden = hidden + dot(x_ref[:, cols], w[0:384, :], 1, 1)
        grad_active = grad_active + dot(g_ref[:, cols], w[384:576, :], 1, 1)
    active, grad_gate, grad_up = swiglu(hidden[:, :192], hidden[:, 192:], grad_active)
    grad_hidden = jnp.concatenate([grad_gate, grad_up], axis=1)
    for b in range(8):
        down = dot(active, g_ref[:, 256 * b : 256 * b + 256], 0, 0).astype(BF)
        for d in range(8):
            t_ref[d, 384 + 24 * b : 408 + 24 * b, :] = down[24 * d : 24 * d + 24, :]
    for d, cols, w in blocks:
        t_ref[d, 0:384, :] = dot(grad_hidden, x_ref[:, cols], 0, 0).astype(BF)
        out = dot(active, w[384:576, :]).astype(BF)
        back = dot(grad_hidden, w[0:384, :]).astype(BF)
        for k, dst in enumerate((mine_ref.at[0], mine_ref.at[1], theirs_ref.at[0], theirs_ref.at[1])):
            dst[0:80, cols] = out[80 * k : 80 * k + 80]
            dst[80:160, cols] = back[80 * k : 80 * k + 80]
    for n, p in enumerate((p0_ref, p1_ref, p2_ref, p3_ref)):
        rows = pl.ds(pl.multiple_of((z + n) % 4 * 144, 16), 144)
        for s in range(4):
            for r in range(2):
                p[r, s] = t_ref[(h if r == 0 else 1 - h) * 4 + (y + s) % 4, rows, :]


def finish_kernel(
    here_ref, spare_ref, more_ref, pick_ref, in_ref, in_got_ref, d0_ref, d1_ref, d2_ref, d3_ref,
    after_ref, out_in_ref, out_down_ref, t_ref,
):
    z, l, c = here_ref[2], here_ref[3], here_ref[4]
    flag = here_ref[5].astype(F32)
    for rc, src in enumerate((spare_ref, more_ref)):
        for rl in range(2):
            q = 2 * (c if rc == 0 else 1 - c) + (l if rl == 0 else 1 - l)
            for s in range(4):
                rows = pl.ds(pl.multiple_of((z + 4 - s) % 4 * 144, 16), 144)
                t_ref[q, rows, :] = src[rl, s]
    pick = pick_ref[...]
    for part in range(2):
        rows = jnp.concatenate(
            [t_ref[q, 192 * part : 192 * part + 192, :] for q in range(4)], axis=0
        )
        cols = slice(768 * part, 768 * part + 768)
        home = in_ref[:, cols].astype(F32) + in_got_ref[:, cols].astype(F32)
        out_in_ref[:, cols] = home + flag * dot(rows, pick, 0, 1)
    for q in range(4):
        for b in range(8):
            rows, cols = slice(24 * q, 24 * q + 24), slice(256 * b, 256 * b + 256)
            home = d0_ref[rows, cols].astype(F32) + d1_ref[rows, cols].astype(F32)
            home = home + d2_ref[rows, cols].astype(F32) + d3_ref[rows, cols].astype(F32)
            piece = t_ref[q, 384 + 24 * b : 408 + 24 * b, :].astype(F32)
            out_down_ref[rows, cols] = home + flag * piece


def shards(tokens, cotangent, route_gates, w_gate_up, w_down, expert_ids, dest_ranks, slot_ids):
    dp, ex = lax.axis_index("dp"), lax.axis_index("expert")
    h, y = dp // 4, dp % 4
    z, l, c = ex // 4, (ex // 2) % 2, ex % 2
    w_in, w_out = w_gate_up[0], w_down[0]
    i32 = jnp.int32

    unit = jnp.arange(768, dtype=i32)
    place = unit % 192 // 24 * 96 + unit // 192 * 24 + unit % 24
    pick = (unit[:, None] == place[None, :]).astype(BF)
    here = jnp.stack([h, y, z, l, c]).astype(i32)
    tables = (expert_ids.T, dest_ranks.T, slot_ids.T, route_gates.T)
    parts, hot_rows, pos, hot = route(here, tables, (tokens, cotangent), (w_in, w_out), pick)
    hot = hot[0, 0]
    hz, hl, hc = hot // 4, (hot // 2) % 2, hot % 2
    here = jnp.concatenate([here, (ex == hot).astype(i32).reshape(1)])

    got = hop(parts[1], dc=1)
    piece = jnp.where(c == hc, parts[0], got)
    near_w = hop(piece[1], dl=1)
    piece = jnp.where(l == hl, piece[0], near_w)
    got = [hop(piece, dz=s) for s in (1, 2, 3)]
    away = (z - hz) % 4
    piece = jnp.where(
        away == 0, piece, jnp.where(away == 1, got[0], jnp.where(away == 2, got[1], got[2]))
    )
    hot_rows = sum_after([hot_rows], [near_w], "keep_rows")
    near_rows = hop(hot_rows, dl=1)
    far_rows = hop(jnp.stack([hot_rows, near_rows]), dc=1)
    piece = jnp.stack([piece, hop(piece, dh=1)])

    (send,) = call(
        pack_kernel,
        "pack_rows",
        (shape(640, 2048),),
        (pos, tables[3], tokens, cotangent, piece, near_rows),
        in_specs=[VMEM] * 4 + [AFTER] * 2,
    )
    recv = lax.all_to_all(send, "expert", split_axis=0, concat_axis=0, tiled=True)
    hot_w = [piece] + [hop(piece, dy=s) for s in (1, 2, 3)]

    mine, theirs, *spares = call(
        hot_kernel,
        "hot_expert",
        (shape(2, 160, 2048), shape(2, 160, 2048)) + (shape(2, 4, 144, 256),) * 4,
        (here, hot_rows, near_rows, far_rows, *hot_w, recv),
        scratch=(
            pltpu.VMEM((320, 2048), BF),
            pltpu.VMEM((320, 2048), BF),
            pltpu.VMEM((8, 576, 256), BF),
        ),
        in_specs=[SMEM] + [VMEM] * 7 + [AFTER],
    )
    mine = total(mine, hop(theirs, dc=1))
    near_part = hop(mine[1], dl=1)

    def picks(rows, stride):
        compact = jnp.arange(rows, dtype=i32)
        spread = compact // 20 * stride + compact % 20
        row = jnp.arange(rows // 20 * stride, dtype=i32)
        return [(spread[:, None] + shift == row).astype(BF) for shift in (0, 20)]

    pick_x, pick_g = picks(80, 40)
    back_x, back_g = picks(320, 40)
    active, grad_hidden, rows_x, rows_g = call(
        home_kernel,
        "home_hidden",
        (shape(320, 768), shape(320, 1536), shape(320, 2048), shape(320, 2048)),
        (recv, pick_x, pick_g, w_in, w_out, spares[0]),
        in_specs=[VMEM] * 5 + [AFTER],
    )
    from_z = [hop(spares[s], dz=s) for s in (1, 2, 3)]
    half = shape(2, 256, 768)
    in_own, up_a, dn_b, to_up, to_dn, out_own, out_far = call(
        grads_kernel,
        "home_grads",
        (shape(2, 256, 1536),) + (half,) * 2 + (shape(2, 2, 256, 768),) * 2 + (shape(4, 96, 2048),) * 2,
        (here, active, grad_hidden, rows_x, rows_g, near_part, from_z[0], from_z[2]),
        in_specs=[SMEM] + [VMEM] * 4 + [AFTER] * 3,
    )
    spare = sum_after(
        [spares[0]] + from_z, [in_own], "sum_z"
    )
    (result,) = call(
        result_kernel,
        "home_rows",
        (shape(640, 2048),),
        (active, grad_hidden, back_x, back_g, w_in, w_out, spare),
        in_specs=[VMEM] * 6 + [AFTER],
    )
    returned = lax.all_to_all(result, "expert", split_axis=0, concat_axis=0, tiled=True)

    from_dn, from_up = hop(to_up, dy=1), hop(to_dn, dy=3)
    out_sum = total(out_own, hop(out_far, dh=1))
    up_a = sum_after([up_a, from_dn[0]], [result], "sum_up")
    dn_b = sum_after([dn_b, from_up[1]], [result], "sum_down")
    spare = sum_after([spare[0], hop(spare[1], dh=1)], [up_a, dn_b], "sum_x")
    up_a, dn_b = hop(up_a, dy=1), hop(dn_b, dy=3)
    up_b, dn_a = from_dn[1], from_up[0]
    in_sum = total(
        in_own, jnp.concatenate([up_a, up_b], axis=2), jnp.concatenate([dn_a, dn_b], axis=2)
    )
    in_got = hop(in_sum[1], dh=1)
    out_parts = [out_sum[0]] + [hop(out_sum[s], dy=s) for s in (1, 2, 3)]
    spare = total(spare[0], *[hop(spare[s], dy=s) for s in (1, 2, 3)])

    mixed, token_grad = call(
        unpack_kernel,
        "unpack_rows",
        (shape(256, 2048), shape(256, 2048)),
        (pos, route_gates, returned, mine, near_part),
    )

    (spare,) = call(
        stack_kernel,
        "stack_z",
        (shape(4, 144, 256),),
        (spare, *[hop(spare, dz=s) for s in (1, 2, 3)], returned, in_got, *out_parts),
        in_specs=[VMEM] * 4 + [AFTER] * 6,
    )
    spare = jnp.stack([spare, hop(spare, dl=1)])
    more = hop(spare, dc=1)
    grad_gate_up, grad_down = call(
        finish_kernel,
        "finish_grads",
        (shape(256, 1536, dtype=F32), shape(96, 2048, dtype=F32)),
        (here, spare, more, pick, in_sum[0], in_got, *out_parts, mixed),
        scratch=(pltpu.VMEM((4, 576, 256), BF),),
        in_specs=[SMEM] + [VMEM] * 9 + [AFTER],
    )
    return mixed, token_grad, grad_gate_up[None], grad_down[None]


def solution(mesh):
    rows = P(AXES, None)
    weights = P("expert", None, None)
    grads = P("expert", "dp", None)
    return jax.shard_map(
        shards,
        mesh=mesh,
        in_specs=(rows, rows, rows, weights, weights, rows, rows, rows),
        out_specs=(rows, rows, grads, grads),
        check_vma=False,
    )
```

```python
import functools

import jax
import jax.numpy as jnp
from jax import lax
from jax.experimental import pallas as pl
from jax.experimental.pallas import tpu as pltpu
from jax.sharding import PartitionSpec as P

AXES = ("dp", "expert")
BF = jnp.bfloat16
F32 = jnp.float32


def hop(x, dh=0, dy=0, dz=0, dl=0, dc=0):
    pairs = []
    for i in range(128):
        dp, ex = divmod(i, 16)
        h, y = divmod(dp, 4)
        z, l, c = ex // 4, (ex // 2) % 2, ex % 2
        j_dp = ((h + dh) % 2) * 4 + (y + dy) % 4
        j_ex = ((z + dz) % 4) * 4 + ((l + dl) % 2) * 2 + (c + dc) % 2
        pairs.append((i, j_dp * 16 + j_ex))
    return lax.ppermute(x, AXES, pairs)


def dot(a, b, ca=1, cb=0):
    return lax.dot_general(a, b, (((ca,), (cb,)), ((), ())), preferred_element_type=F32)


def total(*parts, dtype=BF):
    out = parts[0].astype(F32)
    for part in parts[1:]:
        out = out + part.astype(F32)
    return out.astype(dtype)


VMEM = pl.BlockSpec(memory_space=pltpu.VMEM)
SMEM = pl.BlockSpec(memory_space=pltpu.SMEM)
AFTER = pl.BlockSpec(memory_space=pl.ANY)


def call(kernel, name, outs, args, scratch=(), in_specs=None, out_specs=None):
    return pl.pallas_call(
        kernel,
        out_shape=outs,
        in_specs=in_specs or [VMEM] * len(args),
        out_specs=out_specs or (VMEM,) * len(outs),
        scratch_shapes=list(scratch),
        compiler_params=pltpu.CompilerParams(vmem_limit_bytes=48 * 2**20),
        cost_estimate=pl.CostEstimate(flops=10**6, bytes_accessed=10**5, transcendentals=0),
        name=name,
    )(*args)


def shape(*dims, dtype=BF):
    return jax.ShapeDtypeStruct(dims, dtype)


def sum_kernel(count, *refs):
    out = refs[0][...].astype(F32)
    for ref in refs[1:count]:
        out = out + ref[...].astype(F32)
    refs[-1][...] = out.astype(BF)


def stack_kernel(*refs):
    for k in range(4):
        refs[-1][k] = refs[k][...]


def sum_after(parts, after, name):
    return call(
        functools.partial(sum_kernel, len(parts)),
        name,
        (shape(*parts[0].shape),),
        (*parts, *after),
        in_specs=[VMEM] * len(parts) + [AFTER] * len(after),
    )[0]


def select(pos, gates, rows, shift):
    row = lax.broadcasted_iota(jnp.int32, (rows, 256), 0) + shift
    m0 = row == pos[0:1, :]
    m1 = row == pos[1:2, :]
    pick = jnp.where(m0 | m1, 1.0, 0.0).astype(BF)
    gate = jnp.where(m0, gates[0:1, :], 0.0) + jnp.where(m1, gates[1:2, :], 0.0)
    return pick, jnp.sum(gate, axis=1, keepdims=True)


def route_kernel(
    here_ref, ids_ref, dest_ref, slot_ref, gate_ref, tok_ref, cot_ref, in_ref, out_ref, pick_ref,
    parts_ref, hot_ref, pos_ref, top_ref,
):
    l, c = here_ref[3], here_ref[4]
    pick = pick_ref[...]
    gate_w = dot(pick, in_ref[:, :768], 0, 1).astype(BF)
    up_w = dot(pick, in_ref[:, 768:], 0, 1).astype(BF)
    down_w = dot(pick, out_ref[...], 0, 0).astype(BF)
    for q in range(4):
        units = slice(192 * q, 192 * q + 192)
        rows = jnp.concatenate([gate_w[units], up_w[units], down_w[units]], axis=0)
        parts_ref[(q // 2 + c) % 2, (q % 2 + l) % 2] = rows

    ids, dest, slot = ids_ref[...], dest_ref[...], slot_ref[...]
    served = slot >= 0
    replica = served & (ids != dest)
    top_ref[0, 0] = jnp.max(jnp.where(replica, ids, -1))
    order = jnp.zeros_like(dest)
    for e in range(15):
        found = jnp.where(replica & (dest == e), 1, 0)
        found = jnp.max(jnp.max(found, axis=1, keepdims=True), axis=0, keepdims=True)
        order = order + jnp.where(dest > e, found, 0)
    pos = jnp.where(replica, 640 + order * 20 + slot, dest * 40 + slot)
    pos = jnp.where(served, pos, -1000)
    pos_ref[...] = pos
    hot_x, hot_gate = select(pos, gate_ref[...], 80, 640)
    for j in range(4):
        cols = pl.ds(j * 512, 512)
        hot_ref[0:80, cols] = dot(hot_x, tok_ref[:, cols]).astype(BF)
        hot_ref[80:160, cols] = (hot_gate * dot(hot_x, cot_ref[:, cols])).astype(BF)


def route(here, tables, rows, weights, pick):
    i32 = jnp.int32
    whole = lambda *dims: pl.BlockSpec(dims, lambda i, d: (0,) * len(dims))
    return pl.pallas_call(
        route_kernel,
        out_shape=(
            shape(2, 2, 576, 256),
            shape(160, 2048),
            shape(2, 256, dtype=i32),
            shape(1, 1, dtype=i32),
        ),
        grid_spec=pltpu.PrefetchScalarGridSpec(
            num_scalar_prefetch=1,
            grid=(1,),
            in_specs=[whole(2, 256)] * 4
            + [whole(256, 2048)] * 2
            + [
                pl.BlockSpec((256, 1536), lambda i, d: (d[0] * 4 + d[1], 0)),
                pl.BlockSpec((768, 256), lambda i, d: (0, d[0] * 4 + d[1])),
                whole(768, 768),
            ],
            out_specs=(whole(2, 2, 576, 256), whole(160, 2048), whole(2, 256), SMEM),
        ),
        compiler_params=pltpu.CompilerParams(vmem_limit_bytes=40 * 2**20),
        cost_estimate=pl.CostEstimate(flops=10**6, bytes_accessed=10**5, transcendentals=0),
        name="route",
    )(here, *tables, *rows, *weights, pick)


def pack_kernel(pos_ref, gate_ref, tok_ref, cot_ref, *refs):
    send_ref = refs[-1]
    home_x, _ = select(pos_ref[...], gate_ref[...], 640, 0)
    home_g, home_gate = select(pos_ref[...], gate_ref[...], 640, -20)
    for j in range(4):
        cols = pl.ds(j * 512, 512)
        rows = dot(home_x, tok_ref[:, cols]) + home_gate * dot(home_g, cot_ref[:, cols])
        send_ref[:, cols] = rows.astype(BF)


def unpack_kernel(pos_ref, gate_ref, ret_ref, hot_a_ref, hot_b_ref, mixed_ref, grad_ref):
    def select(k, rows, shift):
        row = lax.broadcasted_iota(jnp.int32, (rows, 256), 0) + shift
        return jnp.where(row == pos_ref[k : k + 1, :], 1.0, 0.0).astype(BF)

    out0, out1 = select(0, 640, 0), select(1, 640, 0)
    back = select(0, 640, -20) + select(1, 640, -20)
    hot0, hot1 = select(0, 80, 640), select(1, 80, 640)
    hot_back = hot0 + hot1
    gate0, gate1 = gate_ref[:, 0:1], gate_ref[:, 1:2]
    for j in range(4):
        cols = pl.ds(j * 512, 512)
        ret = ret_ref[:, cols]
        hot = (hot_a_ref[0, :, cols].astype(F32) + hot_b_ref[:, cols].astype(F32)).astype(BF)
        first = dot(out0, ret, 0, 0) + dot(hot0, hot[:80], 0, 0)
        second = dot(out1, ret, 0, 0) + dot(hot1, hot[:80], 0, 0)
        mixed_ref[:, cols] = (gate0 * first + gate1 * second).astype(BF)
        grads = dot(back, ret, 0, 0) + dot(hot_back, hot[80:], 0, 0)
        grad_ref[:, cols] = grads.astype(BF)


def swiglu(gate, up, grad_active):
    sig = 1.0 / (1.0 + jnp.exp(-gate))
    silu = gate * sig
    active = silu * up
    grad_gate = grad_active * up * sig * (1.0 + gate * (1.0 - sig))
    return active.astype(BF), grad_gate.astype(BF), (grad_active * silu).astype(BF)


def home_kernel(
    recv_ref, pick_x_ref, pick_g_ref, in_ref, out_ref, after_ref, act_ref, gh_ref, x_ref, g_ref
):
    for k in range(4):
        recv = recv_ref[160 * k : 160 * k + 160, :]
        x_ref[80 * k : 80 * k + 80, :] = dot(pick_x_ref[...], recv).astype(BF)
        g_ref[80 * k : 80 * k + 80, :] = dot(pick_g_ref[...], recv).astype(BF)

    def unit_tile(n, carry):
        lo = pl.ds(pl.multiple_of(n * 256, 256), 256)
        hi = pl.ds(pl.multiple_of(768 + n * 256, 256), 256)
        gate = dot(x_ref[...], in_ref[:, lo])
        up = dot(x_ref[...], in_ref[:, hi])
        grad_active = dot(g_ref[...], out_ref[lo, :], 1, 1)
        active, grad_gate, grad_up = swiglu(gate, up, grad_active)
        act_ref[:, lo] = active
        gh_ref[:, lo] = grad_gate
        gh_ref[:, hi] = grad_up
        return carry

    lax.fori_loop(0, 3, unit_tile, 0)


def grads_kernel(here_ref, act_ref, gh_ref, x_ref, g_ref, *refs):
    own_ref, up_ref, dn_ref, to_up_ref, to_dn_ref, out_own_ref, out_far_ref = refs[-7:]
    h, y = here_ref[0], here_ref[1]
    pieces = (
        (own_ref, own_ref),
        (up_ref, to_up_ref.at[1]),
        (to_up_ref.at[0], to_dn_ref.at[1]),
        (to_dn_ref.at[0], dn_ref),
    )

    def side(r, carry):
        hh = h + r - 2 * h * r
        for s, (first, second) in enumerate(pieces):
            block = hh * 4 + (y + s) % 4
            rows = x_ref[:, pl.ds(pl.multiple_of(block * 256, 256), 256)]
            grad = dot(rows, gh_ref[...], 0, 0).astype(BF)
            if s == 0:
                own_ref[r] = grad
            else:
                first[r] = grad[:, :768]
                second[r] = grad[:, 768:]
        return carry

    lax.fori_loop(0, 2, side, 0)
    for r, dst in enumerate((out_own_ref, out_far_ref)):
        hh = h if r == 0 else 1 - h
        units = act_ref[:, pl.ds(pl.multiple_of(hh * 384, 128), 384)]
        for j in range(4):
            cols = pl.ds(j * 512, 512)
            grad = dot(units, g_ref[:, cols], 0, 0).astype(BF)
            for k in range(4):
                dst[(k + 4 - y) % 4, :, cols] = grad[96 * k : 96 * k + 96]


def result_kernel(
    act_ref, gh_ref, pick_x_ref, pick_g_ref, in_ref, out_ref, after_ref, res_ref
):
    def tile(j, carry):
        cols = pl.ds(pl.multiple_of(j * 512, 512), 512)
        out = dot(act_ref[...], out_ref[:, cols]).astype(BF)
        back = dot(gh_ref[...], in_ref[cols, :], 1, 1).astype(BF)
        both_rows = dot(pick_x_ref[...], out, 0, 0) + dot(pick_g_ref[...], back, 0, 0)
        res_ref[:, cols] = both_rows.astype(BF)
        return carry

    lax.fori_loop(0, 4, tile, 0)


def hot_kernel(
    here_ref, own_ref, near_ref, far_ref, w0_ref, w1_ref, w2_ref, w3_ref, after_ref,
    mine_ref, theirs_ref, p0_ref, p1_ref, p2_ref, p3_ref, x_ref, g_ref, t_ref,
):
    h, y, z = here_ref[0], here_ref[1], here_ref[2]
    for k, rows in enumerate((own_ref, near_ref, far_ref.at[0], far_ref.at[1])):
        x_ref[80 * k : 80 * k + 80, :] = rows[0:80, :]
        g_ref[80 * k : 80 * k + 80, :] = rows[80:160, :]
    blocks = []
    for s, w in enumerate((w0_ref, w1_ref, w2_ref, w3_ref)):
        for r in range(2):
            d = (h if r == 0 else 1 - h) * 4 + (y + 4 - s) % 4
            blocks.append((d, pl.ds(pl.multiple_of(d * 256, 256), 256), w.at[r]))
    hidden = jnp.zeros((320, 384), F32)
    grad_active = jnp.zeros((320, 192), F32)
    for d, cols, w in blocks:
        hidden = hidden + dot(x_ref[:, cols], w[0:384, :], 1, 1)
        grad_active = grad_active + dot(g_ref[:, cols], w[384:576, :], 1, 1)
    active, grad_gate, grad_up = swiglu(hidden[:, :192], hidden[:, 192:], grad_active)
    grad_hidden = jnp.concatenate([grad_gate, grad_up], axis=1)
    for b in range(8):
        down = dot(active, g_ref[:, 256 * b : 256 * b + 256], 0, 0).astype(BF)
        for d in range(8):
            t_ref[d, 384 + 24 * b : 408 + 24 * b, :] = down[24 * d : 24 * d + 24, :]
    for d, cols, w in blocks:
        t_ref[d, 0:384, :] = dot(grad_hidden, x_ref[:, cols], 0, 0).astype(BF)
        out = dot(active, w[384:576, :]).astype(BF)
        back = dot(grad_hidden, w[0:384, :]).astype(BF)
        for k, dst in enumerate((mine_ref.at[0], mine_ref.at[1], theirs_ref.at[0], theirs_ref.at[1])):
            dst[0:80, cols] = out[80 * k : 80 * k + 80]
            dst[80:160, cols] = back[80 * k : 80 * k + 80]
    for n, p in enumerate((p0_ref, p1_ref, p2_ref, p3_ref)):
        rows = pl.ds(pl.multiple_of((z + n) % 4 * 144, 16), 144)
        for s in range(4):
            for r in range(2):
                p[r, s] = t_ref[(h if r == 0 else 1 - h) * 4 + (y + s) % 4, rows, :]


def finish_kernel(
    here_ref, spare_ref, more_ref, pick_ref, in_ref, in_got_ref, d0_ref, d1_ref, d2_ref, d3_ref,
    after_ref, out_in_ref, out_down_ref, t_ref,
):
    z, l, c = here_ref[2], here_ref[3], here_ref[4]
    flag = here_ref[5].astype(F32)
    for rc, src in enumerate((spare_ref, more_ref)):
        for rl in range(2):
            q = 2 * (c if rc == 0 else 1 - c) + (l if rl == 0 else 1 - l)
            for s in range(4):
                rows = pl.ds(pl.multiple_of((z + 4 - s) % 4 * 144, 16), 144)
                t_ref[q, rows, :] = src[rl, s]
    pick = pick_ref[...]
    for part in range(2):
        rows = jnp.concatenate(
            [t_ref[q, 192 * part : 192 * part + 192, :] for q in range(4)], axis=0
        )
        cols = slice(768 * part, 768 * part + 768)
        home = in_ref[:, cols].astype(F32) + in_got_ref[:, cols].astype(F32)
        out_in_ref[:, cols] = home + flag * dot(rows, pick, 0, 1)
    for q in range(4):
        for b in range(8):
            rows, cols = slice(24 * q, 24 * q + 24), slice(256 * b, 256 * b + 256)
            home = d0_ref[rows, cols].astype(F32) + d1_ref[rows, cols].astype(F32)
            home = home + d2_ref[rows, cols].astype(F32) + d3_ref[rows, cols].astype(F32)
            piece = t_ref[q, 384 + 24 * b : 408 + 24 * b, :].astype(F32)
            out_down_ref[rows, cols] = home + flag * piece


def shards(tokens, cotangent, route_gates, w_gate_up, w_down, expert_ids, dest_ranks, slot_ids):
    dp, ex = lax.axis_index("dp"), lax.axis_index("expert")
    h, y = dp // 4, dp % 4
    z, l, c = ex // 4, (ex // 2) % 2, ex % 2
    w_in, w_out = w_gate_up[0], w_down[0]
    i32 = jnp.int32

    unit = jnp.arange(768, dtype=i32)
    place = unit % 192 // 24 * 96 + unit // 192 * 24 + unit % 24
    pick = (unit[:, None] == place[None, :]).astype(BF)
    here = jnp.stack([h, y, z, l, c]).astype(i32)
    tables = (expert_ids.T, dest_ranks.T, slot_ids.T, route_gates.T)
    parts, hot_rows, pos, hot = route(here, tables, (tokens, cotangent), (w_in, w_out), pick)
    hot = hot[0, 0]
    hz, hl, hc = hot // 4, (hot // 2) % 2, hot % 2
    here = jnp.concatenate([here, (ex == hot).astype(i32).reshape(1)])

    got = hop(parts[1], dc=1)
    piece = jnp.where(c == hc, parts[0], got)
    near_w = hop(piece[1], dl=1)
    piece = jnp.where(l == hl, piece[0], near_w)
    got = [hop(piece, dz=s) for s in (1, 2, 3)]
    away = (z - hz) % 4
    piece = jnp.where(
        away == 0, piece, jnp.where(away == 1, got[0], jnp.where(away == 2, got[1], got[2]))
    )
    hot_rows = sum_after([hot_rows], [near_w], "keep_rows")
    near_rows = hop(hot_rows, dl=1)
    far_rows = hop(jnp.stack([hot_rows, near_rows]), dc=1)
    piece = jnp.stack([piece, hop(piece, dh=1)])

    (send,) = call(
        pack_kernel,
        "pack_rows",
        (shape(640, 2048),),
        (pos, tables[3], tokens, cotangent, piece, near_rows),
        in_specs=[VMEM] * 4 + [AFTER] * 2,
    )
    recv = lax.all_to_all(send, "expert", split_axis=0, concat_axis=0, tiled=True)
    hot_w = [piece] + [hop(piece, dy=s) for s in (1, 2, 3)]

    mine, theirs, *spares = call(
        hot_kernel,
        "hot_expert",
        (shape(2, 160, 2048), shape(2, 160, 2048)) + (shape(2, 4, 144, 256),) * 4,
        (here, hot_rows, near_rows, far_rows, *hot_w, recv),
        scratch=(
            pltpu.VMEM((320, 2048), BF),
            pltpu.VMEM((320, 2048), BF),
            pltpu.VMEM((8, 576, 256), BF),
        ),
        in_specs=[SMEM] + [VMEM] * 7 + [AFTER],
    )
    mine = total(mine, hop(theirs, dc=1))
    near_part = hop(mine[1], dl=1)

    def picks(rows, stride):
        compact = jnp.arange(rows, dtype=i32)
        spread = compact // 20 * stride + compact % 20
        row = jnp.arange(rows // 20 * stride, dtype=i32)
        return [(spread[:, None] + shift == row).astype(BF) for shift in (0, 20)]

    pick_x, pick_g = picks(80, 40)
    back_x, back_g = picks(320, 40)
    active, grad_hidden, rows_x, rows_g = call(
        home_kernel,
        "home_hidden",
        (shape(320, 768), shape(320, 1536), shape(320, 2048), shape(320, 2048)),
        (recv, pick_x, pick_g, w_in, w_out, spares[0]),
        in_specs=[VMEM] * 5 + [AFTER],
    )
    from_z = [hop(spares[s], dz=s) for s in (1, 2, 3)]
    half = shape(2, 256, 768)
    in_own, up_a, dn_b, to_up, to_dn, out_own, out_far = call(
        grads_kernel,
        "home_grads",
        (shape(2, 256, 1536),) + (half,) * 2 + (shape(2, 2, 256, 768),) * 2 + (shape(4, 96, 2048),) * 2,
        (here, active, grad_hidden, rows_x, rows_g, near_part, from_z[0], from_z[2]),
        in_specs=[SMEM] + [VMEM] * 4 + [AFTER] * 3,
    )
    spare = sum_after(
        [spares[0]] + from_z, [in_own], "sum_z"
    )
    (result,) = call(
        result_kernel,
        "home_rows",
        (shape(640, 2048),),
        (active, grad_hidden, back_x, back_g, w_in, w_out, spare),
        in_specs=[VMEM] * 6 + [AFTER],
    )
    returned = lax.all_to_all(result, "expert", split_axis=0, concat_axis=0, tiled=True)

    from_dn, from_up = hop(to_up, dy=1), hop(to_dn, dy=3)
    out_sum = total(out_own, hop(out_far, dh=1))
    up_a = sum_after([up_a, from_dn[0]], [result], "sum_up")
    dn_b = sum_after([dn_b, from_up[1]], [result], "sum_down")
    spare = sum_after([spare[0], hop(spare[1], dh=1)], [up_a, dn_b], "sum_x")
    up_a, dn_b = hop(up_a, dy=1), hop(dn_b, dy=3)
    up_b, dn_a = from_dn[1], from_up[0]
    in_sum = total(
        in_own, jnp.concatenate([up_a, up_b], axis=2), jnp.concatenate([dn_a, dn_b], axis=2)
    )
    in_got = hop(in_sum[1], dh=1)
    out_parts = [out_sum[0]] + [hop(out_sum[s], dy=s) for s in (1, 2, 3)]
    spare = total(spare[0], *[hop(spare[s], dy=s) for s in (1, 2, 3)])

    mixed, token_grad = call(
        unpack_kernel,
        "unpack_rows",
        (shape(256, 2048), shape(256, 2048)),
        (pos, route_gates, returned, mine, near_part),
    )

    (spare,) = call(
        stack_kernel,
        "stack_z",
        (shape(4, 144, 256),),
        (spare, *[hop(spare, dz=s) for s in (1, 2, 3)], mixed, in_got, *out_parts),
        in_specs=[VMEM] * 4 + [AFTER] * 6,
    )
    spare = jnp.stack([spare, hop(spare, dl=1)])
    more = hop(spare, dc=1)
    grad_gate_up, grad_down = call(
        finish_kernel,
        "finish_grads",
        (shape(256, 1536, dtype=F32), shape(96, 2048, dtype=F32)),
        (here, spare, more, pick, in_sum[0], in_got, *out_parts, mixed),
        scratch=(pltpu.VMEM((4, 576, 256), BF),),
        in_specs=[SMEM] + [VMEM] * 9 + [AFTER],
    )
    return mixed, token_grad, grad_gate_up[None], grad_down[None]


def solution(mesh):
    rows = P(AXES, None)
    weights = P("expert", None, None)
    grads = P("expert", "dp", None)
    return jax.shard_map(
        shards,
        mesh=mesh,
        in_specs=(rows, rows, rows, weights, weights, rows, rows, rows),
        out_specs=(rows, rows, grads, grads),
        check_vma=False,
    )
```
